512 devices in a mesh: dx: 32 (over z_lo, y), dy: 16 (over x, z_hi, core).
Axes of the slice: x: 4, y: 4, z: 16 (z_hi: 2, z_lo: 8; z = z_hi * 8 + z_lo), core: 2. Of those that a mesh axis runs over, the one named last changes fastest.
Arguments:
- query_hidden: bfloat16 [8192, 4096], P(('dx', 'dy')), as said below
- passage_hidden: bfloat16 [65536, 4096], P(('dx', 'dy')), as said below
- gain: float32 [4096], replicated, may hold values from 0.5 to 1.5
- hard_ids: int32 [8192, 7], P(('dx', 'dy')), may hold values from 0 to 4095, as said below
- positive_ids: int32 [8192], P(('dx', 'dy')), may hold values from 0 to 4095, as said below
Outputs:
- query_grad: bfloat16 [8192, 4096], P(('dx', 'dy'))
- passage_grad: bfloat16 [65536, 4096], P(('dx', 'dy'))
- gain_grad: float32 [4096], replicated
- loss: float32 [], replicated
The draws below stay inside these ranges and needn't reach their ends.
Inputs may be any that keep to these rules, and one draw needn't show every extreme that they name: `query_hidden`: final-layer hidden states of order one. `passage_hidden`: final-layer hidden states of order one. `hard_ids`: the query of row r of device x of a group owns the 8 passage positions x * 128 + 8 * r to x * 128 + 8 * r + 7; its positive and its 7 hard negatives are these positions, each once. `positive_ids`: one of the query's own passage positions, as described for hard_ids.
All inputs are finite; a program needn't handle non-finite values.
Results may differ from the reference program's by a relative error of at most 0.017.
Values may be sent and summed in bfloat16 or wider, within the bound.
A program may use at most 64 MiB of HBM per device.

```python
import jax
import jax.numpy as jnp
from jax import lax

D = 4096
Q_DEV = 16
HARD = 7
P_DEV = 128
GROUP_Q = 512
GROUP_P = 4096
QUERIES = 8192
PASSAGES = 65536
N_DX = 32
N_DY = 16


def shared_rows(key):
    return jax.random.normal(key, (PASSAGES, D), jnp.float32)


def own_orders(key):
    key = jax.random.fold_in(key, 5)
    owned = HARD + 1
    rows = jnp.arange(QUERIES, dtype=jnp.int32)
    device = rows // Q_DEV
    local = rows % Q_DEV
    x_pos = device // N_DY
    start = x_pos * P_DEV + owned * local
    ranks = jax.random.randint(key, (QUERIES, owned), 0, 1 << 20, jnp.int32) * owned + jnp.arange(owned, dtype=jnp.int32)[None, :]
    order = jnp.argsort(ranks, axis=1).astype(jnp.int32)
    return start[:, None] + order


def draw_hard_ids(key, part):
    orders = own_orders(key)
    return orders[:, 1:]


def draw_positive_ids(key, part):
    orders = own_orders(key)
    return orders[:, 0]


def draw_query_hidden(key, part):
    key = jax.random.fold_in(key, 11)
    noise_key = jax.random.fold_in(key, 0)
    noise = jax.random.normal(noise_key, (QUERIES, D), jnp.float32)
    result = noise
    return result.astype(jnp.bfloat16)


def draw_passage_hidden(key, part):
    base = shared_rows(key)
    result = base
    return result.astype(jnp.bfloat16)


def setup_inputs(seed: int = 0) -> dict:
    seeds = jax.random.split(jax.random.key(seed), 6)
    return {
        "query_hidden": draw_query_hidden(jax.random.fold_in(seeds[5], 71), 0),
        "passage_hidden": draw_passage_hidden(jax.random.fold_in(seeds[5], 71), 0),
        "gain": jnp.clip(1.0 + 0.1 * jax.random.normal(seeds[2], (D,), jnp.float32), 0.5, 1.5),
        "hard_ids": draw_hard_ids(jax.random.fold_in(seeds[5], 71), 0),
        "positive_ids": draw_positive_ids(jax.random.fold_in(seeds[5], 71), 0),
    }


logit_scale = 250.0
hard_weight = 3.0

def embed(hidden, gain):
    values = hidden.astype(jnp.float32)
    inv_rms = lax.rsqrt(lax.optimization_barrier(jnp.mean(values * values, axis=-1, keepdims=True)) + 1e-05)
    unit = values * inv_rms
    normed = unit * gain
    inv_len = lax.rsqrt(lax.optimization_barrier(jnp.sum(normed * normed, axis=-1, keepdims=True)) + 1e-06)
    return ((normed * inv_len).astype(jnp.bfloat16), unit, normed, inv_len, inv_rms)

def backward(dembed, unit, normed, inv_len, inv_rms, gain):
    unit_embed = normed * inv_len
    dnormed = inv_len * (dembed - unit_embed * lax.optimization_barrier(jnp.sum(unit_embed * dembed, axis=-1, keepdims=True)))
    gain_part = lax.optimization_barrier(jnp.sum(dnormed * unit, axis=0))
    dunit = dnormed * gain
    grad = inv_rms * (dunit - unit * lax.optimization_barrier(jnp.mean(dunit * unit, axis=-1, keepdims=True)))
    return (grad.astype(jnp.bfloat16), gain_part)

def reference(query_hidden, passage_hidden, gain, hard_ids, positive_ids):
    q_emb, q_unit, q_normed, q_inv, q_rms = embed(query_hidden, gain)
    p_emb, p_unit, p_normed, p_inv, p_rms = embed(passage_hidden, gain)
    q_groups = q_emb.reshape(N_DX, N_DY, Q_DEV, D).transpose(1, 0, 2, 3).reshape(N_DY, GROUP_Q, D)
    p_groups = p_emb.reshape(N_DX, N_DY, P_DEV, D).transpose(1, 0, 2, 3).reshape(N_DY, GROUP_P, D)
    hard_groups = hard_ids.reshape(N_DX, N_DY, Q_DEV, HARD).transpose(1, 0, 2, 3).reshape(N_DY, GROUP_Q, HARD)
    pos_groups = positive_ids.reshape(N_DX, N_DY, Q_DEV).transpose(1, 0, 2).reshape(N_DY, GROUP_Q)
    col_ids = jnp.arange(GROUP_P, dtype=jnp.int32)

    def step(loss_total, item):
        q_rows, p_rows, hard_rows, pos_rows = item
        scores = logit_scale * lax.dot_general(q_rows, p_rows, (((1,), (1,)), ((), ())), preferred_element_type=jnp.float32)
        counts = jnp.zeros(scores.shape, jnp.float32)
        for k in range(HARD):
            counts = counts + (hard_rows[:, k:k + 1] == col_ids[None, :]).astype(jnp.float32)
        weights = 1.0 + hard_weight * counts
        is_pos = pos_rows[:, None] == col_ids[None, :]
        top = lax.optimization_barrier(jnp.max(scores, axis=1, keepdims=True))
        total = lax.optimization_barrier(jnp.sum(weights * jnp.exp(scores - top), axis=1, keepdims=True))
        log_total = top + jnp.log(total)
        pos_score = lax.optimization_barrier(jnp.sum(jnp.where(is_pos, scores, 0.0), axis=1))
        dscore = (weights * jnp.exp(scores - log_total) - is_pos.astype(jnp.float32)).astype(jnp.bfloat16)
        grouped = dscore.astype(jnp.float32).reshape(GROUP_Q, N_DX, P_DEV)
        p_blocks = p_rows.astype(jnp.float32).reshape(N_DX, P_DEV, D)
        dq_terms = logit_scale * jnp.einsum('qxp,xpd->qxd', grouped, p_blocks)
        dq_terms = lax.optimization_barrier(dq_terms.astype(jnp.bfloat16)).astype(jnp.float32)
        dq_rows = lax.optimization_barrier(jnp.sum(dq_terms, axis=1))
        dp_rows = logit_scale * lax.dot_general(dscore, q_rows, (((0,), (0,)), ((), ())), preferred_element_type=jnp.float32)
        loss_total = loss_total + jnp.sum(log_total[:, 0] - pos_score)
        return (loss_total, (dq_rows, dp_rows))
    loss, (dq_stack, dp_stack) = lax.scan(step, jnp.zeros((), jnp.float32), (q_groups, p_groups, hard_groups, pos_groups))
    dq_all = dq_stack.reshape(N_DY, N_DX, Q_DEV, D).transpose(1, 0, 2, 3).reshape(QUERIES, D)
    dp_all = dp_stack.reshape(N_DY, N_DX, P_DEV, D).transpose(1, 0, 2, 3).reshape(PASSAGES, D)
    query_grad, q_gain = backward(dq_all, q_unit, q_normed, q_inv, q_rms, gain)
    passage_grad, p_gain = backward(dp_all, p_unit, p_normed, p_inv, p_rms, gain)
    return (query_grad, passage_grad, q_gain + p_gain, loss)
```

```python
import jax
import jax.numpy as jnp
from jax import lax
from jax.experimental import pallas as pl
from jax.experimental.pallas import tpu as pltpu
from jax.sharding import PartitionSpec as P

MESH = pl.DeviceIdType.MESH
F32 = jnp.float32
BF16 = jnp.bfloat16

LOGIT_SCALE = 250.0
HARD_WEIGHT = 3.0
D = 4096
QB = 16
PB = 128
RING = 8
CLASS = 16
NQ = QB * CLASS
NP = 2 * PB
NF = 4
FC = D // NF
SEG = D // CLASS


def kernel(
    q_ref, p_ref, gain_ref, pos_ref,
    qg_ref, pg_ref, gg_ref, loss_ref,
    qb, pb, sc, ds, dq, yr, zs, zr, dp, dps, dpr, dfin, pstat, stats, ga, gar, gb, gbr, gc, gd,
    agz_s, agz_r, agy_s, agy_r, px_s, px_r, st_s, st_r, rsy_s, rsy_r, rsz_s, rsz_r, dp_s, dp_r,
    ga_s, ga_r, gb_s, gb_r, gc_s, gc_r, gd_s, gd_r,
):
    dx = lax.axis_index("dx")
    dy = lax.axis_index("dy")
    y = dx % 4
    z = dx // 4
    half = z // 2
    r = half + (z % 2) * (7 - 2 * half)
    c = y // 2
    cls = (y + c) % 2
    ci = c * RING + r

    def z_of(place):
        return 2 * place + (place // 4) * (15 - 4 * place)

    nxt = z_of((r + 1) % RING) * 4 + y
    yp = z * 4 + 3 - y
    pp = z * 4 + y + 1 - 2 * (y % 2)

    def peer(k):
        other = (ci + k) % CLASS
        c2 = other // RING
        return z_of(other % RING) * 4 + cls + c2 * (3 - 2 * cls)

    def rows(block, size=QB):
        return pl.ds(pl.multiple_of(block * size, size), size)

    def remote(src, dst, send, recv, dev):
        return pltpu.make_async_remote_copy(
            src_ref=src, dst_ref=dst, send_sem=send, recv_sem=recv, device_id=dev, device_id_type=MESH
        )

    barrier = pltpu.get_barrier_semaphore()

    def greet(k, _):
        pl.semaphore_signal(barrier, inc=1, device_id=(peer(k), dy), device_id_type=MESH)
        pl.semaphore_signal(barrier, inc=1, device_id=(dx, (dy + k) % 16), device_id_type=MESH)
        return 0

    lax.fori_loop(1, 16, greet, 0)
    pl.semaphore_signal(barrier, inc=1, device_id=(pp, dy), device_id_type=MESH)

    def embed(hidden):
        v = hidden.astype(F32)
        vg = v * gain_ref[...]
        inv_rms = lax.rsqrt(jnp.sum(v * v, axis=1, keepdims=True) * (1.0 / D) + 1e-05)
        inv_len = lax.rsqrt(jnp.sum(vg * vg, axis=1, keepdims=True) * (inv_rms * inv_rms) + 1e-06)
        return v, vg * (inv_rms * inv_len), inv_rms, inv_len

    _, q_e, _, _ = embed(q_ref[...])
    for f in range(NF):
        qb[f, rows(ci), :] = q_e[:, f * FC:(f + 1) * FC].astype(BF16)

    pl.semaphore_wait(barrier, 31)

    def agz(s, f):
        block = qb.at[f, rows(c * RING + (r - s + RING) % RING), :]
        return remote(block, block, agz_s.at[s, f], agz_r.at[s + 1, f], (nxt, dy))

    def agz_got(s, f):
        block = qb.at[f, rows(c * RING + (r - s + RING) % RING), :]
        return remote(block, block, agz_s.at[s, f], agz_r.at[s, f], (nxt, dy))

    def agy(s, f):
        block = qb.at[f, rows(c * RING + (r - s + RING) % RING), :]
        return remote(block, block, agy_s.at[s, f], agy_r.at[s, f], (yp, dy))

    def agy_got(s, f):
        block = qb.at[f, rows((1 - c) * RING + (r - s + RING) % RING), :]
        return remote(block, block, agy_s.at[s, f], agy_r.at[s, f], (yp, dy))

    for f in range(NF):
        agz(0, f).start()
        agy(0, f).start()

    def embed_block(b, _):
        _, e, inv_rms, inv_len = embed(p_ref[rows(b), :])
        for f in range(NF):
            pb[f, rows(b), :] = e[:, f * FC:(f + 1) * FC].astype(BF16)
        pstat[0, rows(b), :] = inv_rms
        pstat[1, rows(b), :] = inv_len
        return 0

    lax.fori_loop(0, PB // QB, embed_block, 0)

    def swap(f):
        return remote(pb.at[f, pl.ds(0, PB), :], pb.at[f, pl.ds(PB, PB), :], px_s.at[f], px_r.at[f], (pp, dy))

    for f in range(NF):
        swap(f).start()

    def ag_step(s, _):
        for f in range(NF):
            agz_got(s, f).wait_recv()
            agz(s, f).start()
            agy(s, f).start()
        return 0

    lax.fori_loop(1, RING - 1, ag_step, 0)
    for f in range(NF):
        agz_got(RING - 1, f).wait_recv()
        agy(RING - 1, f).start()

    for f in range(NF):
        def got(s, _, f=f):
            agy_got(s, f).wait_recv()
            return 0

        lax.fori_loop(0, RING, got, 0)
        swap(f).wait_recv()
        part = lax.dot_general(pb[f], qb[f], (((1,), (1,)), ((), ())), preferred_element_type=F32)
        sc[...] = part if f == 0 else sc[...] + part
    sc[...] = sc[...] * LOGIT_SCALE

    lane = lax.broadcasted_iota(jnp.int32, (PB, NQ), 1)
    row = lax.broadcasted_iota(jnp.int32, (PB, NQ), 0)
    own = (lane == ci * QB + row // 8).astype(F32)
    ids = lax.broadcasted_iota(jnp.int32, (PB, QB), 0) + dx * PB
    flag = jnp.sum((ids == pos_ref[...]).astype(F32), axis=1, keepdims=True)
    is_pos = own * flag
    weights = 1.0 + HARD_WEIGHT * (own - is_pos)

    s_own = sc[0:PB, :]
    s_far = sc[PB:NP, :]
    top = jnp.maximum(jnp.max(s_own, axis=0, keepdims=True), jnp.max(s_far, axis=0, keepdims=True))
    total = jnp.sum(weights * jnp.exp(s_own - top), axis=0, keepdims=True) + jnp.sum(
        jnp.exp(s_far - top), axis=0, keepdims=True
    )
    stats[ci, 0:1, :] = top
    stats[ci, 1:2, :] = total

    def stat(k):
        return remote(stats.at[ci], stats.at[ci], st_s.at[k], st_r.at[k], (peer(k), dy))

    def stat_got(k):
        slot = stats.at[(ci - k + CLASS) % CLASS]
        return remote(slot, slot, st_s.at[k], st_r.at[k], (peer(k), dy))

    def start_stat(k, _):
        stat(k).start()
        return 0

    def wait_stat(k, _):
        stat_got(k).wait_recv()
        return 0

    lax.fori_loop(1, CLASS, start_stat, 0)
    pos_score = jnp.sum(is_pos * s_own, axis=0, keepdims=True)
    lax.fori_loop(1, CLASS, wait_stat, 0)
    top_all = stats[0, 0:1, :]
    for k in range(1, CLASS):
        top_all = jnp.maximum(top_all, stats[k, 0:1, :])
    sum_all = jnp.zeros((1, NQ), F32)
    for k in range(CLASS):
        sum_all = sum_all + stats[k, 1:2, :] * jnp.exp(stats[k, 0:1, :] - top_all)
    log_total = top_all + jnp.log(sum_all)
    lane1 = lax.broadcasted_iota(jnp.int32, (1, NQ), 1)
    loss_part = jnp.sum(
        jnp.where(lane1 // QB == ci, log_total - pos_score, 0.0), axis=1, keepdims=True
    )

    ds[0:PB, :] = (weights * jnp.exp(s_own - log_total) - is_pos).astype(BF16)
    ds[PB:NP, :] = jnp.exp(s_far - log_total).astype(BF16)
    ds_f = ds[...].astype(F32)
    ds_t = jnp.transpose(ds_f).astype(BF16)
    prod = ds_f * sc[...]
    u = jnp.sum(prod, axis=1, keepdims=True)
    t_row = jnp.sum(prod, axis=0, keepdims=True)
    t = jnp.transpose(jnp.broadcast_to(t_row, (8, NQ)))[:, 0:1]

    def dest(j):
        return (r + 2 * RING - 1 - j) % RING

    def rsy(j, f):
        return remote(
            dq.at[f, rows((1 - c) * RING + dest(j)), :], yr.at[j, f], rsy_s.at[j, f], rsy_r.at[j, f], (yp, dy)
        )

    def rsz(j, f):
        return remote(zs.at[j, f], zr.at[j + 1, f], rsz_s.at[j, f], rsz_r.at[j + 1, f], (nxt, dy))

    def rsz_got(j, f):
        return remote(zs.at[j, f], zr.at[j, f], rsz_s.at[j, f], rsz_r.at[j, f], (nxt, dy))

    def send_dp(f):
        return remote(dps.at[f], dpr.at[f], dp_s.at[f], dp_r.at[f], (pp, dy))

    for f in range(NF):
        dq[f] = (LOGIT_SCALE * jnp.dot(ds_t, pb[f], preferred_element_type=F32)).astype(BF16)

        def start_rsy(j, _, f=f):
            rsy(j, f).start()
            return 0

        lax.fori_loop(0, RING, start_rsy, 0)

    def ring_step(j, _):
        for f in range(NF):
            rsy(j, f).wait_recv()
            rsz_got(j, f).wait_recv()
            own_part = dq[f, rows(c * RING + dest(j)), :].astype(F32)
            zs[j, f] = (own_part + yr[j, f].astype(F32) + zr[j, f].astype(F32)).astype(BF16)
            rsz(j, f).start()
        return 0

    for f in range(NF):
        rsy(0, f).wait_recv()
        own_part = dq[f, rows(c * RING + dest(0)), :].astype(F32)
        zs[0, f] = (own_part + yr[0, f].astype(F32)).astype(BF16)
        rsz(0, f).start()

    for f in range(NF):
        d = LOGIT_SCALE * jnp.dot(ds[...], qb[f], preferred_element_type=F32)
        dp[f] = d[0:PB, :]
        dps[f] = d[PB:NP, :].astype(BF16)
        send_dp(f).start()
        p_e = pb[f].astype(F32)
        q_f = qb[f].astype(F32)
        g = jnp.sum(p_e * (2.0 * d - p_e * u), axis=0, keepdims=True) - jnp.sum(
            q_f * q_f * t, axis=0, keepdims=True
        )
        g = g / gain_ref[:, f * FC:(f + 1) * FC]
        for k in range(FC // SEG):
            ga[f * (FC // SEG) + k, 0:1, :] = g[:, k * SEG:(k + 1) * SEG]
            ga[f * (FC // SEG) + k, 1:2, :] = jnp.broadcast_to(loss_part, (1, SEG))
        ring_step(f + 1, 0)

    def seg_to(k):
        return remote(ga.at[(ci + k) % CLASS], gar.at[ci], ga_s.at[k], ga_r.at[k], (peer(k), dy))

    def seg_got(k):
        slot = gar.at[(ci - k + CLASS) % CLASS]
        return remote(slot, slot, ga_s.at[k], ga_r.at[k], (peer(k), dy))

    def pair():
        return remote(gb, gbr, gb_s, gb_r, (pp, dy))

    def over_dy(k):
        return remote(gc.at[dy], gc.at[dy], gc_s.at[k], gc_r.at[k], (dx, (dy + k) % 16))

    def over_dy_got(k):
        slot = gc.at[(dy - k + 16) % 16]
        return remote(slot, slot, gc_s.at[k], gc_r.at[k], (dx, (dy + k) % 16))

    def back(k):
        return remote(gd.at[ci], gd.at[ci], gd_s.at[k], gd_r.at[k], (peer(k), dy))

    def back_got(k):
        slot = gd.at[(ci - k + CLASS) % CLASS]
        return remote(slot, slot, gd_s.at[k], gd_r.at[k], (peer(k), dy))

    def each(make, act):
        def body(k, _):
            copy = make(k)
            if act == "start":
                copy.start()
            elif act == "recv":
                copy.wait_recv()
            else:
                copy.wait_send()
            return 0

        lax.fori_loop(1, 16, body, 0)

    each(seg_to, "start")
    gar[ci] = ga[ci]
    ring_step(5, 0)
    each(seg_got, "recv")
    seg = gar[0]
    for k in range(1, CLASS):
        seg = seg + gar[k]
    gb[...] = seg
    pair().start()
    ring_step(6, 0)
    pair().wait_recv()
    gc[dy] = gb[...] + gbr[...]
    each(over_dy, "start")

    for f in range(NF):
        send_dp(f).wait_recv()

    def backward(hidden, inv_rms, inv_len, d):
        g = gain_ref[...]
        unit = hidden.astype(F32) * inv_rms
        e = unit * g * inv_len
        dnormed = inv_len * (d - e * jnp.sum(e * d, axis=1, keepdims=True))
        dunit = dnormed * g
        mean = jnp.sum(dunit * unit, axis=1, keepdims=True) * (1.0 / D)
        return (inv_rms * (dunit - unit * mean)).astype(BF16)

    def p_block(b, _):
        at = rows(b)
        d = jnp.concatenate([dp[f, at, :] + dpr[f, at, :].astype(F32) for f in range(NF)], axis=1)
        pg_ref[at, :] = backward(p_ref[at, :], pstat[0, at, :], pstat[1, at, :], d)
        return 0

    lax.fori_loop(0, PB // QB // 2, p_block, 0)
    each(over_dy_got, "recv")
    seg = gc[0]
    for k in range(1, 16):
        seg = seg + gc[k]
    gd[ci] = seg
    each(back, "start")
    lax.fori_loop(PB // QB // 2, PB // QB, p_block, 0)

    for f in range(NF):
        rsy(RING - 1, f).wait_recv()
        rsz_got(RING - 1, f).wait_recv()
        dfin[:, f * FC:(f + 1) * FC] = (
            dq[f, rows(c * RING + r), :].astype(F32) + yr[RING - 1, f].astype(F32) + zr[RING - 1, f].astype(F32)
        )
    _, _, q_rms, q_len = embed(q_ref[...])
    qg_ref[...] = backward(q_ref[...], q_rms, q_len, dfin[...])

    each(back_got, "recv")
    for k in range(CLASS):
        gg_ref[:, k * SEG:(k + 1) * SEG] = gd[k, 0:1, :]
    loss_ref[...] = gd[0, 1:2, 0:1]

    def done(s, _):
        for f in range(NF):
            agz(s, f).wait_send()
            rsz(s, f).wait_send()
        return 0

    def done_y(s, _):
        for f in range(NF):
            agy(s, f).wait_send()
            rsy(s, f).wait_send()
        return 0

    lax.fori_loop(0, RING - 1, done, 0)
    lax.fori_loop(0, RING, done_y, 0)
    for f in range(NF):
        swap(f).wait_send()
        send_dp(f).wait_send()
    each(stat, "send")
    each(seg_to, "send")
    pair().wait_send()
    each(over_dy, "send")
    each(back, "send")


def on_device(query_hidden, passage_hidden, gain, hard_ids, positive_ids):
    del hard_ids
    vmem = pl.BlockSpec(memory_space=pltpu.VMEM)
    dma = pltpu.SemaphoreType.DMA
    query_grad, passage_grad, gain_grad, loss = pl.pallas_call(
        kernel,
        out_shape=(
            jax.ShapeDtypeStruct((QB, D), BF16),
            jax.ShapeDtypeStruct((PB, D), BF16),
            jax.ShapeDtypeStruct((1, D), F32),
            jax.ShapeDtypeStruct((1, 1), F32),
        ),
        in_specs=[vmem] * 4,
        out_specs=(vmem,) * 4,
        scratch_shapes=[
            pltpu.VMEM((NF, NQ, FC), BF16),
            pltpu.VMEM((NF, NP, FC), BF16),
            pltpu.VMEM((NP, NQ), F32),
            pltpu.VMEM((NP, NQ), BF16),
            pltpu.VMEM((NF, NQ, FC), BF16),
            pltpu.VMEM((RING, NF, QB, FC), BF16),
            pltpu.VMEM((RING, NF, QB, FC), BF16),
            pltpu.VMEM((RING, NF, QB, FC), BF16),
            pltpu.VMEM((NF, PB, FC), F32),
            pltpu.VMEM((NF, PB, FC), BF16),
            pltpu.VMEM((NF, PB, FC), BF16),
            pltpu.VMEM((QB, D), F32),
            pltpu.VMEM((2, PB, 1), F32),
            pltpu.VMEM((CLASS, 2, NQ), F32),
            pltpu.VMEM((CLASS, 2, SEG), F32),
            pltpu.VMEM((CLASS, 2, SEG), F32),
            pltpu.VMEM((2, SEG), F32),
            pltpu.VMEM((2, SEG), F32),
            pltpu.VMEM((16, 2, SEG), F32),
            pltpu.VMEM((CLASS, 2, SEG), F32),
            dma((RING, NF)), dma((RING, NF)),
            dma((RING, NF)), dma((RING, NF)),
            dma((NF,)), dma((NF,)),
            dma((CLASS,)), dma((CLASS,)),
            dma((RING, NF)), dma((RING, NF)),
            dma((RING, NF)), dma((RING, NF)),
            dma((NF,)), dma((NF,)),
            dma((CLASS,)), dma((CLASS,)),
            dma, dma,
            dma((16,)), dma((16,)),
            dma((CLASS,)), dma((CLASS,)),
        ],
        compiler_params=pltpu.CompilerParams(
            collective_id=0, has_side_effects=True, vmem_limit_bytes=40 * 1024 * 1024
        ),
        cost_estimate=pl.CostEstimate(flops=1_610_612_736, bytes_accessed=2_400_000, transcendentals=200_000),
    )(query_hidden, passage_hidden, gain.reshape(1, D), positive_ids.reshape(1, QB))
    return query_grad, passage_grad, gain_grad.reshape(D), loss.reshape(())


def solution(mesh):
    placed = (
        P(("dx", "dy"), None),
        P(("dx", "dy"), None),
        P(),
        P(("dx", "dy"), None),
        P(("dx", "dy")),
    )
    return jax.shard_map(
        on_device,
        mesh=mesh,
        in_specs=placed,
        out_specs=(P(("dx", "dy"), None), P(("dx", "dy"), None), P(), P()),
        check_vma=False,
    )
```

```python
import jax
import jax.numpy as jnp
from jax import lax
from jax.experimental import pallas as pl
from jax.experimental.pallas import tpu as pltpu
from jax.sharding import PartitionSpec as P

MESH = pl.DeviceIdType.MESH
F32 = jnp.float32
BF16 = jnp.bfloat16

LOGIT_SCALE = 250.0
HARD_WEIGHT = 3.0
D = 4096
QB = 16
PB = 128
RING = 8
CLASS = 16
NQ = QB * CLASS
NP = 2 * PB
NF = 4
FC = D // NF
SEG = D // CLASS


def kernel(
    q_hbm, p_hbm, gain_hbm, pos_hbm,
    qg_ref, pg_ref, gg_ref, loss_ref,
    q_ref, p_ref, gain_ref, pos_ref,
    qb, pb, sc, ds, dq, yr, zs, zr, dp, dps, dpr, dfin, pstat, stats, ga, gar, gb, gbr, gc, gd,
    in_sem, z_r, rsy_r, dp_r, agy_r, one_s, one_r,
):
    dx = lax.axis_index("dx")
    dy = lax.axis_index("dy")
    y = dx % 4
    z = dx // 4
    half = z // 2
    r = half + (z % 2) * (7 - 2 * half)
    c = y // 2
    cls = (y + c) % 2
    ci = c * RING + r

    def z_of(place):
        return 2 * place + (place // 4) * (15 - 4 * place)

    nxt = z_of((r + 1) % RING) * 4 + y
    prv = z_of((r + RING - 1) % RING) * 4 + y
    yp = z * 4 + 3 - y
    pp = z * 4 + y + 1 - 2 * (y % 2)

    def peer(k):
        other = (ci + k) % CLASS
        c2 = other // RING
        return z_of(other % RING) * 4 + cls + c2 * (3 - 2 * cls)

    def rows(block, size=QB):
        return pl.ds(pl.multiple_of(block * size, size), size)

    def remote(src, dst, send, recv, dev, other_dy=None):
        return pltpu.make_async_remote_copy(
            src_ref=src, dst_ref=dst, send_sem=send, recv_sem=recv,
            device_id=(dev, dy if other_dy is None else other_dy), device_id_type=MESH,
        )

    loads = [
        pltpu.make_async_copy(src, dst, in_sem.at[i])
        for i, (src, dst) in enumerate(
            ((q_hbm, q_ref), (gain_hbm, gain_ref), (pos_hbm, pos_ref), (p_hbm, p_ref))
        )
    ]
    for load in loads:
        load.start()

    barrier = pltpu.get_barrier_semaphore()

    def greet(k, _):
        pl.semaphore_signal(barrier, inc=1, device_id=(peer(k), dy), device_id_type=MESH)
        pl.semaphore_signal(barrier, inc=1, device_id=(dx, (dy + k) % 16), device_id_type=MESH)
        return 0

    lax.fori_loop(1, 16, greet, 0)
    pl.semaphore_signal(barrier, inc=1, device_id=(pp, dy), device_id_type=MESH)

    def embed(hidden):
        v = hidden.astype(F32)
        vg = v * gain_ref[...]
        inv_rms = lax.rsqrt(jnp.sum(v * v, axis=1, keepdims=True) * (1.0 / D) + 1e-05)
        inv_len = lax.rsqrt(jnp.sum(vg * vg, axis=1, keepdims=True) * (inv_rms * inv_rms) + 1e-06)
        return vg * (inv_rms * inv_len), inv_rms, inv_len

    loads[0].wait()
    loads[1].wait()
    q_e, _, _ = embed(q_ref[...])
    for f in range(NF):
        qb[f, rows(ci), :] = q_e[:, f * FC:(f + 1) * FC].astype(BF16)

    pl.semaphore_wait(barrier, 31)

    def block(off, f, cc=None):
        return qb.at[f, rows((c if cc is None else cc) * RING + (r + off + RING) % RING), :]

    def send_f(h, f):
        return remote(block(-h, f), block(-h, f), one_s.at[0], z_r.at[2 * h, f], nxt)

    def send_b(h, f):
        return remote(block(h, f), block(h, f), one_s.at[0], z_r.at[2 * h + 1, f], prv)

    def got_f(h, f):
        return remote(block(-h, f), block(-h, f), one_s.at[0], z_r.at[2 * h - 2, f], nxt)

    def got_b(h, f):
        return remote(block(h, f), block(h, f), one_s.at[0], z_r.at[2 * h - 1, f], prv)

    def send_y(off, f):
        return remote(block(off, f), block(off, f), one_s.at[1], agy_r.at[f], yp)

    for f in range(NF):
        send_f(0, f).start()
        send_b(0, f).start()
        send_y(0, f).start()

    loads[3].wait()

    def embed_block(b, _):
        e, inv_rms, inv_len = embed(p_ref[rows(b), :])
        for f in range(NF):
            pb[f, rows(b), :] = e[:, f * FC:(f + 1) * FC].astype(BF16)
        pstat[0, rows(b), :] = inv_rms
        pstat[1, rows(b), :] = inv_len
        remote(pb.at[:, rows(b), :], pb.at[:, rows(b + PB // QB), :], one_s.at[2], one_r.at[2], pp).start()
        return 0

    lax.fori_loop(0, PB // QB, embed_block, 0)

    loads[2].wait()
    lane = lax.broadcasted_iota(jnp.int32, (PB, NQ), 1)
    row = lax.broadcasted_iota(jnp.int32, (PB, NQ), 0)
    own = (lane == ci * QB + row // 8).astype(F32)
    ids = lax.broadcasted_iota(jnp.int32, (PB, QB), 0) + dx * PB
    flag = jnp.sum((ids == pos_ref[...]).astype(F32), axis=1, keepdims=True)

    for h in range(1, 5):
        for f in range(NF):
            forth = f < NF // 2
            if h < 4 or forth:
                got_f(h, f).wait_recv()
                if h < 3 or (h == 3 and forth):
                    send_f(h, f).start()
                send_y(-h, f).start()
            if h < 4 or not forth:
                got_b(h, f).wait_recv()
                if h < 3 or (h == 3 and not forth):
                    send_b(h, f).start()
                send_y(h, f).start()

    swapped = pb.at[:, pl.ds(PB, PB), :]
    remote(swapped, swapped, one_s.at[2], one_r.at[2], pp).wait_recv()
    for f in range(NF):
        theirs = qb.at[f, rows(1 - c, RING * QB), :]
        remote(theirs, theirs, one_s.at[1], agy_r.at[f], yp).wait_recv()
        part = lax.dot_general(pb[f], qb[f], (((1,), (1,)), ((), ())), preferred_element_type=F32)
        sc[...] = part if f == 0 else sc[...] + part
    sc[...] = sc[...] * LOGIT_SCALE

    is_pos = own * flag
    weights = 1.0 + HARD_WEIGHT * (own - is_pos)
    s_own = sc[0:PB, :]
    s_far = sc[PB:NP, :]
    top = jnp.maximum(jnp.max(s_own, axis=0, keepdims=True), jnp.max(s_far, axis=0, keepdims=True))
    total = jnp.sum(weights * jnp.exp(s_own - top), axis=0, keepdims=True) + jnp.sum(
        jnp.exp(s_far - top), axis=0, keepdims=True
    )
    stats[ci, 0:1, :] = top
    stats[ci, 1:2, :] = total

    def to_class(ref_of, dst, i):
        def go(k, _):
            remote(ref_of(k), dst.at[ci], one_s.at[i], one_r.at[i], peer(k)).start()
            return 0

        lax.fori_loop(1, CLASS, go, 0)

    def fifteen(ref, i):
        part = ref.at[pl.ds(0, 15)]
        return remote(part, part, one_s.at[i], one_r.at[i], pp)

    to_class(lambda k: stats.at[ci], stats, 3)
    pos_score = jnp.sum(is_pos * s_own, axis=0, keepdims=True)
    fifteen(stats, 3).wait_recv()
    top_all = stats[0, 0:1, :]
    for k in range(1, CLASS):
        top_all = jnp.maximum(top_all, stats[k, 0:1, :])
    sum_all = jnp.zeros((1, NQ), F32)
    for k in range(CLASS):
        sum_all = sum_all + stats[k, 1:2, :] * jnp.exp(stats[k, 0:1, :] - top_all)
    log_total = top_all + jnp.log(sum_all)
    lane1 = lax.broadcasted_iota(jnp.int32, (1, NQ), 1)
    loss_part = jnp.sum(
        jnp.where(lane1 // QB == ci, log_total - pos_score, 0.0), axis=1, keepdims=True
    )

    ds[0:PB, :] = (weights * jnp.exp(s_own - log_total) - is_pos).astype(BF16)
    ds[PB:NP, :] = jnp.exp(s_far - log_total).astype(BF16)
    ds_f = ds[...].astype(F32)
    ds_t = jnp.transpose(ds_f).astype(BF16)

    offs = (4, 3, -3, 2, -2, 1, -1, 0)
    slot_after = (None, 3, 4, 5, 6, 7, 0)

    def dest(i, cc):
        return rows(cc * RING + (r + offs[i] + RING) % RING)

    for f in range(NF):
        dq[f] = (LOGIT_SCALE * jnp.dot(ds_t, pb[f], preferred_element_type=F32)).astype(BF16)
    for i in range(RING):
        for f in range(NF):
            remote(dq.at[f, dest(i, 1 - c), :], yr.at[i, f], one_s.at[4], rsy_r.at[i, f], yp).start()

    for f in range(NF):
        d = LOGIT_SCALE * jnp.dot(ds[...], qb[f], preferred_element_type=F32)
        dp[:, f * FC:(f + 1) * FC] = d[0:PB, :]
        dps[:, f * FC:(f + 1) * FC] = d[PB:NP, :].astype(BF16)

    def send_dp(b):
        return remote(dps.at[rows(b), :], dpr.at[rows(b), :], one_s.at[5], dp_r.at[b], pp)

    def start_dp(b, _):
        send_dp(b).start()
        return 0

    lax.fori_loop(0, PB // QB, start_dp, 0)

    def zr_got(i, f):
        return remote(zs.at[0, f], zr.at[i, f], one_s.at[6], z_r.at[i, f], nxt)

    def ring_step(i):
        for f in range(NF):
            forth = f < NF // 2
            rsy = remote(yr.at[i, f], yr.at[i, f], one_s.at[4], rsy_r.at[i, f], yp)
            rsy.wait_recv()
            acc = dq[f, dest(i, c), :].astype(F32) + yr[i, f].astype(F32)
            if i >= 3 or (i == 1 and forth) or (i == 2 and not forth):
                zr_got(i, f).wait_recv()
                acc = acc + zr[i, f].astype(F32)
            zs[i, f] = acc.astype(BF16)
            ahead = forth if i == 0 else i % 2 == 1
            after = (1 if forth else 2) if i == 0 else slot_after[i]
            remote(zs.at[i, f], zr.at[after, f], one_s.at[6], z_r.at[after, f], nxt if ahead else prv).start()

    ring_step(0)

    prod = ds_f * sc[...]
    u = jnp.sum(prod, axis=1, keepdims=True)
    t_row = jnp.sum(prod, axis=0, keepdims=True)
    t = jnp.transpose(jnp.broadcast_to(t_row, (8, NQ)))[:, 0:1]
    for f in range(NF):
        cols = slice(f * FC, (f + 1) * FC)
        p_own = pb[f, 0:PB, :].astype(F32)
        p_far = pb[f, PB:NP, :].astype(F32)
        q_f = qb[f].astype(F32)
        g = (
            jnp.sum(p_own * (2.0 * dp[:, cols] - p_own * u[0:PB]), axis=0, keepdims=True)
            + jnp.sum(p_far * (2.0 * dps[:, cols].astype(F32) - p_far * u[PB:NP]), axis=0, keepdims=True)
            - jnp.sum(q_f * q_f * t, axis=0, keepdims=True)
        ) / gain_ref[:, cols]
        for k in range(FC // SEG):
            ga[f * (FC // SEG) + k, 0:1, :] = g[:, k * SEG:(k + 1) * SEG]
            ga[f * (FC // SEG) + k, 1:2, :] = jnp.broadcast_to(loss_part, (1, SEG))

    ring_step(1)
    ring_step(2)

    to_class(lambda k: ga.at[(ci + k) % CLASS], gar, 7)
    gar[ci] = ga[ci]

    def backward(hidden, inv_rms, inv_len, d):
        g = gain_ref[...]
        unit = hidden.astype(F32) * inv_rms
        e = unit * g * inv_len
        dnormed = inv_len * (d - e * jnp.sum(e * d, axis=1, keepdims=True))
        dunit = dnormed * g
        mean = jnp.sum(dunit * unit, axis=1, keepdims=True) * (1.0 / D)
        return (inv_rms * (dunit - unit * mean)).astype(BF16)

    def p_block(b, _):
        send_dp(b).wait_recv()
        at = rows(b)
        d = dp[at, :] + dpr[at, :].astype(F32)
        pg_ref[at, :] = backward(p_ref[at, :], pstat[0, at, :], pstat[1, at, :], d)
        return 0

    def p_blocks(b0, b1):
        lax.fori_loop(b0, b1, p_block, 0)

    p_blocks(0, 1)
    ring_step(3)
    ring_step(4)

    fifteen(gar, 7).wait_recv()
    seg = gar[0]
    for k in range(1, CLASS):
        seg = seg + gar[k]
    gb[...] = seg
    pair = remote(gb, gbr, one_s.at[8], one_r.at[8], pp)
    pair.start()
    p_blocks(1, 3)
    ring_step(5)
    ring_step(6)

    pair.wait_recv()
    gc[dy] = gb[...] + gbr[...]

    def over_dy(k, _):
        remote(gc.at[dy], gc.at[dy], one_s.at[9], one_r.at[9], dx, (dy + k) % 16).start()
        return 0

    lax.fori_loop(1, 16, over_dy, 0)
    p_blocks(3, 5)
    fifteen(gc, 9).wait_recv()
    seg = gc[0]
    for k in range(1, 16):
        seg = seg + gc[k]
    gd[ci] = seg
    to_class(lambda k: gd.at[ci], gd, 10)
    p_blocks(5, 6)

    for f in range(NF):
        rsy = remote(yr.at[RING - 1, f], yr.at[RING - 1, f], one_s.at[4], rsy_r.at[RING - 1, f], yp)
        rsy.wait_recv()
        zr_got(7, f).wait_recv()
        zr_got(0, f).wait_recv()
        dfin[:, f * FC:(f + 1) * FC] = (
            dq[f, dest(7, c), :].astype(F32) + yr[RING - 1, f].astype(F32)
            + (zr[7, f].astype(F32) + zr[0, f].astype(F32))
        )
    _, q_rms, q_len = embed(q_ref[...])
    qg_ref[...] = backward(q_ref[...], q_rms, q_len, dfin[...])
    p_blocks(6, 8)

    fifteen(gd, 10).wait_recv()
    for k in range(CLASS):
        gg_ref[:, k * SEG:(k + 1) * SEG] = gd[k, 0:1, :]
    loss_ref[...] = gd[0, 1:2, 0:1]

    for ref, i in (
        (qb.at[:, pl.ds(0, 7 * QB), :], 0), (qb.at[:, pl.ds(0, 8 * QB), :], 1), (swapped, 2),
        (yr, 4), (dpr, 5), (zs.at[pl.ds(0, 7)], 6), (gb, 8),
    ):
        remote(ref, ref, one_s.at[i], one_r.at[i], pp).wait_send()
    for ref, i in ((stats, 3), (gar, 7), (gc, 9), (gd, 10)):
        fifteen(ref, i).wait_send()


def on_device(query_hidden, passage_hidden, gain, hard_ids, positive_ids):
    del hard_ids
    vmem = pl.BlockSpec(memory_space=pltpu.VMEM)
    hbm = pl.BlockSpec(memory_space=pl.ANY)
    dma = pltpu.SemaphoreType.DMA
    query_grad, passage_grad, gain_grad, loss = pl.pallas_call(
        kernel,
        out_shape=(
            jax.ShapeDtypeStruct((QB, D), BF16),
            jax.ShapeDtypeStruct((PB, D), BF16),
            jax.ShapeDtypeStruct((1, D), F32),
            jax.ShapeDtypeStruct((1, 1), F32),
        ),
        in_specs=[hbm] * 4,
        out_specs=(vmem,) * 4,
        scratch_shapes=[
            pltpu.VMEM((QB, D), BF16),
            pltpu.VMEM((PB, D), BF16),
            pltpu.VMEM((1, D), F32),
            pltpu.VMEM((1, QB), jnp.int32),
            pltpu.VMEM((NF, NQ, FC), BF16),
            pltpu.VMEM((NF, NP, FC), BF16),
            pltpu.VMEM((NP, NQ), F32),
            pltpu.VMEM((NP, NQ), BF16),
            pltpu.VMEM((NF, NQ, FC), BF16),
            pltpu.VMEM((RING, NF, QB, FC), BF16),
            pltpu.VMEM((RING, NF, QB, FC), BF16),
            pltpu.VMEM((RING, NF, QB, FC), BF16),
            pltpu.VMEM((PB, D), F32),
            pltpu.VMEM((PB, D), BF16),
            pltpu.VMEM((PB, D), BF16),
            pltpu.VMEM((QB, D), F32),
            pltpu.VMEM((2, PB, 1), F32),
            pltpu.VMEM((CLASS, 2, NQ), F32),
            pltpu.VMEM((CLASS, 2, SEG), F32),
            pltpu.VMEM((CLASS, 2, SEG), F32),
            pltpu.VMEM((2, SEG), F32),
            pltpu.VMEM((2, SEG), F32),
            pltpu.VMEM((16, 2, SEG), F32),
            pltpu.VMEM((CLASS, 2, SEG), F32),
            dma((4,)),
            dma((RING, NF)),
            dma((RING, NF)),
            dma((PB // QB,)),
            dma((NF,)),
            dma((11,)),
            dma((11,)),
        ],
        compiler_params=pltpu.CompilerParams(
            collective_id=0, has_side_effects=True, vmem_limit_bytes=40 * 1024 * 1024
        ),
        cost_estimate=pl.CostEstimate(flops=1_610_612_736, bytes_accessed=2_400_000, transcendentals=200_000),
    )(query_hidden, passage_hidden, gain.reshape(1, D), positive_ids.reshape(1, QB))
    return query_grad, passage_grad, gain_grad.reshape(D), loss.reshape(())


def solution(mesh):
    placed = (
        P(("dx", "dy"), None),
        P(("dx", "dy"), None),
        P(),
        P(("dx", "dy"), None),
        P(("dx", "dy")),
    )
    return jax.shard_map(
        on_device,
        mesh=mesh,
        in_specs=placed,
        out_specs=(P(("dx", "dy"), None), P(("dx", "dy"), None), P(), P()),
        check_vma=False,
    )
```

```python
import jax
import jax.numpy as jnp
from jax import lax
from jax.experimental import pallas as pl
from jax.experimental.pallas import tpu as pltpu
from jax.sharding import PartitionSpec as P

MESH = pl.DeviceIdType.MESH
F32 = jnp.float32
BF16 = jnp.bfloat16

LOGIT_SCALE = 250.0
HARD_WEIGHT = 3.0
D = 4096
QB = 16
PB = 128
RING = 8
CLASS = 16
NQ = QB * CLASS
NP = 2 * PB
NF = 4
FC = D // NF
SEG = D // CLASS


def kernel(
    q_hbm, p_hbm, gain_hbm, pos_hbm,
    qg_ref, pg_ref, gg_ref, loss_ref,
    q_ref, p_ref, gain_ref, pos_ref,
    qb, pb, sc, ds, dq, yr, zs, zr, dp, dps, dpr, dfin, pstat, stats, ga, gar, gb, gbr, gc, gd, et, from_y,
    in_sem, z_r, rsy_r, dp_r, agy_r, one_s, one_r,
):
    dx = lax.axis_index("dx")
    dy = lax.axis_index("dy")
    y = dx % 4
    z = dx // 4
    half = z // 2
    r = half + (z % 2) * (7 - 2 * half)
    c = y // 2
    cls = (y + c) % 2
    ci = c * RING + r

    def z_of(place):
        return 2 * place + (place // 4) * (15 - 4 * place)

    nxt = z_of((r + 1) % RING) * 4 + y
    prv = z_of((r + RING - 1) % RING) * 4 + y
    yp = z * 4 + 3 - y
    pp = z * 4 + y + 1 - 2 * (y % 2)

    def peer(k):
        other = (ci + k) % CLASS
        c2 = other // RING
        return z_of(other % RING) * 4 + cls + c2 * (3 - 2 * cls)

    def rows(block, size=QB):
        return pl.ds(pl.multiple_of(block * size, size), size)

    def remote(src, dst, send, recv, dev, other_dy=None):
        return pltpu.make_async_remote_copy(
            src_ref=src, dst_ref=dst, send_sem=send, recv_sem=recv,
            device_id=(dev, dy if other_dy is None else other_dy), device_id_type=MESH,
        )

    loads = [
        pltpu.make_async_copy(src, dst, in_sem.at[i])
        for i, (src, dst) in enumerate(
            ((q_hbm, q_ref), (gain_hbm, gain_ref), (pos_hbm, pos_ref), (p_hbm, p_ref))
        )
    ]
    for load in loads:
        load.start()

    barrier = pltpu.get_barrier_semaphore()

    def greet(k, _):
        pl.semaphore_signal(barrier, inc=1, device_id=(peer(k), dy), device_id_type=MESH)
        pl.semaphore_signal(barrier, inc=1, device_id=(dx, (dy + k) % 16), device_id_type=MESH)
        return 0

    lax.fori_loop(1, 16, greet, 0)
    pl.semaphore_signal(barrier, inc=1, device_id=(pp, dy), device_id_type=MESH)

    def embed(hidden):
        v = hidden.astype(F32)
        vg = v * gain_ref[...]
        inv_rms = lax.rsqrt(jnp.sum(v * v, axis=1, keepdims=True) * (1.0 / D) + 1e-05)
        inv_len = lax.rsqrt(jnp.sum(vg * vg, axis=1, keepdims=True) * (inv_rms * inv_rms) + 1e-06)
        return vg * (inv_rms * inv_len), inv_rms, inv_len

    loads[0].wait()
    loads[1].wait()
    q_e, _, _ = embed(q_ref[...])
    for f in range(NF):
        qb[f, rows(ci), :] = q_e[:, f * FC:(f + 1) * FC].astype(BF16)

    pl.semaphore_wait(barrier, 31)

    def block(off, f, cc=None):
        return qb.at[f, rows((c if cc is None else cc) * RING + (r + off + RING) % RING), :]

    def send_f(h, f):
        return remote(block(-h, f), block(-h, f), one_s.at[0], z_r.at[2 * h, f], nxt)

    def send_b(h, f):
        return remote(block(h, f), block(h, f), one_s.at[0], z_r.at[2 * h + 1, f], prv)

    def got_f(h, f):
        return remote(block(-h, f), block(-h, f), one_s.at[0], z_r.at[2 * h - 2, f], nxt)

    def got_b(h, f):
        return remote(block(h, f), block(h, f), one_s.at[0], z_r.at[2 * h - 1, f], prv)

    def send_y(off, f):
        return remote(block(off, f), block(off, f), one_s.at[1], agy_r.at[f], yp)

    for f in range(NF):
        send_f(0, f).start()
        send_b(0, f).start()
        send_y(0, f).start()

    loads[3].wait()

    def embed_block(b, _):
        e, inv_rms, inv_len = embed(p_ref[rows(b), :])
        for f in range(NF):
            pb[f, rows(b), :] = e[:, f * FC:(f + 1) * FC].astype(BF16)
        pstat[0, rows(b), :] = inv_rms
        pstat[1, rows(b), :] = inv_len
        remote(pb.at[:, rows(b), :], pb.at[:, rows(b + PB // QB), :], one_s.at[2], one_r.at[2], pp).start()
        return 0

    lax.fori_loop(0, PB // QB, embed_block, 0)

    loads[2].wait()
    lane = lax.broadcasted_iota(jnp.int32, (PB, NQ), 1)
    row = lax.broadcasted_iota(jnp.int32, (PB, NQ), 0)
    own = (lane == ci * QB + row // 8).astype(F32)
    ids = lax.broadcasted_iota(jnp.int32, (PB, QB), 0) + dx * PB
    flag = jnp.sum((ids == pos_ref[...]).astype(F32), axis=1, keepdims=True)

    for h in range(1, 5):
        for f in range(NF):
            forth = f < NF // 2
            if h < 4 or forth:
                got_f(h, f).wait_recv()
                if h < 3 or (h == 3 and forth):
                    send_f(h, f).start()
                send_y(-h, f).start()
            if h < 4 or not forth:
                got_b(h, f).wait_recv()
                if h < 3 or (h == 3 and not forth):
                    send_b(h, f).start()
                send_y(h, f).start()

    swapped = pb.at[:, pl.ds(PB, PB), :]
    remote(swapped, swapped, one_s.at[2], one_r.at[2], pp).wait_recv()
    for f in range(NF):
        arrived = qb.at[f, rows(1 - c, RING * QB), :]
        remote(arrived, arrived, one_s.at[1], agy_r.at[f], yp).wait_recv()
        part = lax.dot_general(pb[f], qb[f], (((1,), (1,)), ((), ())), preferred_element_type=F32)
        sc[...] = part if f == 0 else sc[...] + part
    sc[...] = sc[...] * LOGIT_SCALE

    is_pos = own * flag
    weights = 1.0 + HARD_WEIGHT * (own - is_pos)
    s_own = sc[0:PB, :]
    s_far = sc[PB:NP, :]
    top = jnp.maximum(jnp.max(s_own, axis=0, keepdims=True), jnp.max(s_far, axis=0, keepdims=True))
    e_own = weights * jnp.exp(s_own - top)
    e_far = jnp.exp(s_far - top)
    total = jnp.sum(e_own, axis=0, keepdims=True) + jnp.sum(e_far, axis=0, keepdims=True)
    stats[ci, 0:1, :] = top
    stats[ci, 1:2, :] = total

    def to_class(ref_of, dst, i):
        def go(k, _):
            remote(ref_of(k), dst.at[ci], one_s.at[i], one_r.at[i], peer(k)).start()
            return 0

        lax.fori_loop(1, CLASS, go, 0)

    def fifteen(ref, i):
        part = ref.at[pl.ds(0, 15)]
        return remote(part, part, one_s.at[i], one_r.at[i], pp)

    to_class(lambda k: stats.at[ci], stats, 3)

    offs = (4, 3, -3, 2, -2, 1, -1, 0)
    slot_after = (None, 3, 4, 5, 6, 7, 0)

    def dest(i, cc):
        return rows(cc * RING + (r + offs[i] + RING) % RING)

    et[:, 0:PB] = jnp.transpose(e_own).astype(BF16)
    et[:, PB:NP] = jnp.transpose(e_far).astype(BF16)
    theirs = rows(1 - c, RING * QB)
    for f in range(NF):
        dq[f, theirs, :] = jnp.dot(et[theirs, :], pb[f], preferred_element_type=F32).astype(BF16)
    for i in range(RING):
        for f in range(NF):
            remote(dq.at[f, dest(i, 1 - c), :], yr.at[i, f], one_s.at[4], rsy_r.at[i, f], yp).start()

    pos_score = jnp.sum(is_pos * s_own, axis=0, keepdims=True)
    fifteen(stats, 3).wait_recv()
    top_all = stats[0, 0:1, :]
    for k in range(1, CLASS):
        top_all = jnp.maximum(top_all, stats[k, 0:1, :])
    sum_all = jnp.zeros((1, NQ), F32)
    for k in range(CLASS):
        sum_all = sum_all + stats[k, 1:2, :] * jnp.exp(stats[k, 0:1, :] - top_all)
    log_total = top_all + jnp.log(sum_all)
    lane1 = lax.broadcasted_iota(jnp.int32, (1, NQ), 1)
    loss_part = jnp.sum(
        jnp.where(lane1 // QB == ci, log_total - pos_score, 0.0), axis=1, keepdims=True
    )

    ds[0:PB, :] = (weights * jnp.exp(s_own - log_total) - is_pos).astype(BF16)
    ds[PB:NP, :] = jnp.exp(s_far - log_total).astype(BF16)
    ds_f = ds[...].astype(F32)
    et[...] = jnp.transpose(ds_f).astype(BF16)
    scale = LOGIT_SCALE * jnp.exp(stats[(1 - c) * RING + r, 0:1, :] - log_total)
    from_y[...] = jnp.transpose(jnp.broadcast_to(scale, (8, NQ)))[:, 0:1]

    for f in range(NF):
        d = LOGIT_SCALE * jnp.dot(ds[...], qb[f], preferred_element_type=F32)
        dp[:, f * FC:(f + 1) * FC] = d[0:PB, :]
        dps[:, f * FC:(f + 1) * FC] = d[PB:NP, :].astype(BF16)

    def send_dp(b):
        return remote(dps.at[rows(b), :], dpr.at[rows(b), :], one_s.at[5], dp_r.at[b], pp)

    def start_dp(b, _):
        send_dp(b).start()
        return 0

    lax.fori_loop(0, PB // QB, start_dp, 0)

    ours = rows(c, RING * QB)
    for f in range(NF):
        dq[f, ours, :] = (LOGIT_SCALE * jnp.dot(et[ours, :], pb[f], preferred_element_type=F32)).astype(BF16)

    def zr_got(i, f):
        return remote(zs.at[0, f], zr.at[i, f], one_s.at[6], z_r.at[i, f], nxt)

    def ring_step(i):
        for f in range(NF):
            forth = f < NF // 2
            rsy = remote(yr.at[i, f], yr.at[i, f], one_s.at[4], rsy_r.at[i, f], yp)
            rsy.wait_recv()
            acc = dq[f, dest(i, c), :].astype(F32) + yr[i, f].astype(F32) * from_y[dest(i, c), :]
            if i >= 3 or (i == 1 and forth) or (i == 2 and not forth):
                zr_got(i, f).wait_recv()
                acc = acc + zr[i, f].astype(F32)
            zs[i, f] = acc.astype(BF16)
            ahead = forth if i == 0 else i % 2 == 1
            after = (1 if forth else 2) if i == 0 else slot_after[i]
            remote(zs.at[i, f], zr.at[after, f], one_s.at[6], z_r.at[after, f], nxt if ahead else prv).start()

    prod = ds_f * sc[...]
    u = jnp.sum(prod, axis=1, keepdims=True)
    t_row = jnp.sum(prod, axis=0, keepdims=True)
    t = jnp.transpose(jnp.broadcast_to(t_row, (8, NQ)))[:, 0:1]
    for f in range(NF):
        cols = slice(f * FC, (f + 1) * FC)
        p_own = pb[f, 0:PB, :].astype(F32)
        p_far = pb[f, PB:NP, :].astype(F32)
        q_f = qb[f].astype(F32)
        g = (
            jnp.sum(p_own * (2.0 * dp[:, cols] - p_own * u[0:PB]), axis=0, keepdims=True)
            + jnp.sum(p_far * (2.0 * dps[:, cols].astype(F32) - p_far * u[PB:NP]), axis=0, keepdims=True)
            - jnp.sum(q_f * q_f * t, axis=0, keepdims=True)
        ) / gain_ref[:, cols]
        for k in range(FC // SEG):
            ga[f * (FC // SEG) + k, 0:1, :] = g[:, k * SEG:(k + 1) * SEG]
            ga[f * (FC // SEG) + k, 1:2, :] = jnp.broadcast_to(loss_part, (1, SEG))

    to_class(lambda k: ga.at[(ci + k) % CLASS], gar, 7)
    gar[ci] = ga[ci]

    ring_step(0)
    ring_step(1)
    ring_step(2)

    fifteen(gar, 7).wait_recv()
    seg = gar[0]
    for k in range(1, CLASS):
        seg = seg + gar[k]
    gb[...] = seg
    pair = remote(gb, gbr, one_s.at[8], one_r.at[8], pp)
    pair.start()

    def backward(hidden, inv_rms, inv_len, d):
        g = gain_ref[...]
        unit = hidden.astype(F32) * inv_rms
        e = unit * g * inv_len
        dnormed = inv_len * (d - e * jnp.sum(e * d, axis=1, keepdims=True))
        dunit = dnormed * g
        mean = jnp.sum(dunit * unit, axis=1, keepdims=True) * (1.0 / D)
        return (inv_rms * (dunit - unit * mean)).astype(BF16)

    def p_block(b, _):
        send_dp(b).wait_recv()
        at = rows(b)
        d = dp[at, :] + dpr[at, :].astype(F32)
        pg_ref[at, :] = backward(p_ref[at, :], pstat[0, at, :], pstat[1, at, :], d)
        return 0

    def p_blocks(b0, b1):
        lax.fori_loop(b0, b1, p_block, 0)

    ring_step(3)
    ring_step(4)

    pair.wait_recv()
    gc[dy] = gb[...] + gbr[...]

    def over_dy(k, _):
        remote(gc.at[dy], gc.at[dy], one_s.at[9], one_r.at[9], dx, (dy + k) % 16).start()
        return 0

    lax.fori_loop(1, 16, over_dy, 0)
    p_blocks(0, 2)
    ring_step(5)
    ring_step(6)
    p_blocks(2, 4)

    fifteen(gc, 9).wait_recv()
    seg = gc[0]
    for k in range(1, 16):
        seg = seg + gc[k]
    gd[ci] = seg
    to_class(lambda k: gd.at[ci], gd, 10)
    p_blocks(4, 6)

    for f in range(NF):
        rsy = remote(yr.at[RING - 1, f], yr.at[RING - 1, f], one_s.at[4], rsy_r.at[RING - 1, f], yp)
        rsy.wait_recv()
        zr_got(7, f).wait_recv()
        zr_got(0, f).wait_recv()
        dfin[:, f * FC:(f + 1) * FC] = (
            dq[f, dest(7, c), :].astype(F32) + yr[RING - 1, f].astype(F32) * from_y[dest(7, c), :]
            + (zr[7, f].astype(F32) + zr[0, f].astype(F32))
        )
    _, q_rms, q_len = embed(q_ref[...])
    qg_ref[...] = backward(q_ref[...], q_rms, q_len, dfin[...])
    p_blocks(6, 8)

    fifteen(gd, 10).wait_recv()
    for k in range(CLASS):
        gg_ref[:, k * SEG:(k + 1) * SEG] = gd[k, 0:1, :]
    loss_ref[...] = gd[0, 1:2, 0:1]

    for ref, i in (
        (qb.at[:, pl.ds(0, 7 * QB), :], 0), (qb.at[:, pl.ds(0, 8 * QB), :], 1), (swapped, 2),
        (yr, 4), (dpr, 5), (zs.at[pl.ds(0, 7)], 6), (gb, 8),
    ):
        remote(ref, ref, one_s.at[i], one_r.at[i], pp).wait_send()
    for ref, i in ((stats, 3), (gar, 7), (gc, 9), (gd, 10)):
        fifteen(ref, i).wait_send()


def on_device(query_hidden, passage_hidden, gain, hard_ids, positive_ids):
    del hard_ids
    vmem = pl.BlockSpec(memory_space=pltpu.VMEM)
    hbm = pl.BlockSpec(memory_space=pltpu.HBM)
    dma = pltpu.SemaphoreType.DMA
    query_grad, passage_grad, gain_grad, loss = pl.pallas_call(
        kernel,
        out_shape=(
            jax.ShapeDtypeStruct((QB, D), BF16),
            jax.ShapeDtypeStruct((PB, D), BF16),
            jax.ShapeDtypeStruct((1, D), F32),
            jax.ShapeDtypeStruct((1, 1), F32),
        ),
        in_specs=[hbm] * 4,
        out_specs=(vmem,) * 4,
        scratch_shapes=[
            pltpu.VMEM((QB, D), BF16),
            pltpu.VMEM((PB, D), BF16),
            pltpu.VMEM((1, D), F32),
            pltpu.VMEM((1, QB), jnp.int32),
            pltpu.VMEM((NF, NQ, FC), BF16),
            pltpu.VMEM((NF, NP, FC), BF16),
            pltpu.VMEM((NP, NQ), F32),
            pltpu.VMEM((NP, NQ), BF16),
            pltpu.VMEM((NF, NQ, FC), BF16),
            pltpu.VMEM((RING, NF, QB, FC), BF16),
            pltpu.VMEM((RING, NF, QB, FC), BF16),
            pltpu.VMEM((RING, NF, QB, FC), BF16),
            pltpu.VMEM((PB, D), F32),
            pltpu.VMEM((PB, D), BF16),
            pltpu.VMEM((PB, D), BF16),
            pltpu.VMEM((QB, D), F32),
            pltpu.VMEM((2, PB, 1), F32),
            pltpu.VMEM((CLASS, 2, NQ), F32),
            pltpu.VMEM((CLASS, 2, SEG), F32),
            pltpu.VMEM((CLASS, 2, SEG), F32),
            pltpu.VMEM((2, SEG), F32),
            pltpu.VMEM((2, SEG), F32),
            pltpu.VMEM((16, 2, SEG), F32),
            pltpu.VMEM((CLASS, 2, SEG), F32),
            pltpu.VMEM((NQ, NP), BF16),
            pltpu.VMEM((NQ, 1), F32),
            dma((4,)),
            dma((RING, NF)),
            dma((RING, NF)),
            dma((PB // QB,)),
            dma((NF,)),
            dma((11,)),
            dma((11,)),
        ],
        compiler_params=pltpu.CompilerParams(
            collective_id=0, has_side_effects=True, vmem_limit_bytes=40 * 1024 * 1024
        ),
        cost_estimate=pl.CostEstimate(flops=1_610_612_736, bytes_accessed=2_400_000, transcendentals=200_000),
    )(query_hidden, passage_hidden, gain.reshape(1, D), positive_ids.reshape(1, QB))
    return query_grad, passage_grad, gain_grad.reshape(D), loss.reshape(())


def solution(mesh):
    placed = (
        P(("dx", "dy"), None),
        P(("dx", "dy"), None),
        P(),
        P(("dx", "dy"), None),
        P(("dx", "dy")),
    )
    return jax.shard_map(
        on_device,
        mesh=mesh,
        in_specs=placed,
        out_specs=(P(("dx", "dy"), None), P(("dx", "dy"), None), P(), P()),
        check_vma=False,
    )
```

```python
import jax
import jax.numpy as jnp
from jax import lax
from jax.experimental import pallas as pl
from jax.experimental.pallas import tpu as pltpu
from jax.sharding import PartitionSpec as P

MESH = pl.DeviceIdType.MESH
F32 = jnp.float32
BF16 = jnp.bfloat16

LOGIT_SCALE = 250.0
HARD_WEIGHT = 3.0
D = 4096
QB = 16
PB = 128
RING = 8
CLASS = 16
NQ = QB * CLASS
NP = 2 * PB
NF = 4
FC = D // NF
PLANE = 32
SEG = D // PLANE


def kernel(
    q_hbm, p_hbm, gain_hbm, pos_hbm,
    qg_ref, pg_ref, gg_ref, loss_ref,
    q_ref, p_ref, far_ref, gain_ref, pos_ref,
    qb, pb, sc, ds, dq, yr, zs, zr, dp, dps, dpr, dfin, pstat, stats, ga, gar, gc, gd, et, from_y,
    in_sem, z_r, rsy_r, dp_r, px_r, agy_r, one_s, one_r,
):
    dx = lax.axis_index("dx")
    dy = lax.axis_index("dy")
    y = dx % 4
    z = dx // 4
    half = z // 2
    r = half + (z % 2) * (7 - 2 * half)
    c = y // 2
    cls = (y + c) % 2
    ci = c * RING + r

    def z_of(place):
        return 2 * place + (place // 4) * (15 - 4 * place)

    nxt = z_of((r + 1) % RING) * 4 + y
    prv = z_of((r + RING - 1) % RING) * 4 + y
    yp = z * 4 + 3 - y
    pp = z * 4 + y + 1 - 2 * (y % 2)

    x = dy // 4
    z_hi = (dy // 2) % 2
    core = dy % 2
    plane = (x * 4 + y) * 2 + core
    tall = z_hi * RING + z

    def in_plane(k):
        other = (plane + k) % PLANE
        return z * 4 + (other // 2) % 4, (other // 8) * 4 + z_hi * 2 + other % 2

    def along_z(k):
        other = (tall + k) % 16
        return (other % RING) * 4 + y, x * 4 + (other // RING) * 2 + core

    def in_class(j, cc):
        return z_of((r + j) % RING) * 4 + cls + cc * (3 - 2 * cls)

    def rows(block, size=QB):
        return pl.ds(pl.multiple_of(block * size, size), size)

    def remote(src, dst, send, recv, dev, other_dy=None):
        return pltpu.make_async_remote_copy(
            src_ref=src, dst_ref=dst, send_sem=send, recv_sem=recv,
            device_id=(dev, dy if other_dy is None else other_dy), device_id_type=MESH,
        )

    loads = [
        pltpu.make_async_copy(src, dst, in_sem.at[i])
        for i, (src, dst) in enumerate(
            ((q_hbm, q_ref), (gain_hbm, gain_ref), (pos_hbm, pos_ref), (p_hbm, p_ref))
        )
    ]
    for load in loads:
        load.start()

    barrier = pltpu.get_barrier_semaphore()

    def greet(dev, other_dy):
        pl.semaphore_signal(barrier, inc=1, device_id=(dev, other_dy), device_id_type=MESH)

    def greet_plane(k, _):
        greet(*in_plane(k))
        return 0

    def greet_z(k, _):
        greet(*along_z(k))
        return 0

    def greet_class(k, _):
        greet(in_class(k, 1 - c), dy)
        return 0

    lax.fori_loop(1, 16, greet_z, 0)
    lax.fori_loop(1, RING, greet_class, 0)
    lax.fori_loop(1, PLANE, greet_plane, 0)

    def embed(hidden):
        v = hidden.astype(F32)
        vg = v * gain_ref[...]
        inv_rms = lax.rsqrt(jnp.sum(v * v, axis=1, keepdims=True) * (1.0 / D) + 1e-05)
        inv_len = lax.rsqrt(jnp.sum(vg * vg, axis=1, keepdims=True) * (inv_rms * inv_rms) + 1e-06)
        return vg * (inv_rms * inv_len), inv_rms, inv_len

    loads[0].wait()
    loads[1].wait()
    q_e, _, _ = embed(q_ref[...])
    for f in range(NF):
        qb[f, rows(ci), :] = q_e[:, f * FC:(f + 1) * FC].astype(BF16)

    loads[3].wait()
    pl.semaphore_wait(barrier, 31 + 15 + 7)

    def block(off, f, cc=None):
        return qb.at[f, rows((c if cc is None else cc) * RING + (r + off + RING) % RING), :]

    def send_f(h, f):
        return remote(block(-h, f), block(-h, f), one_s.at[0], z_r.at[2 * h, f], nxt)

    def send_b(h, f):
        return remote(block(h, f), block(h, f), one_s.at[0], z_r.at[2 * h + 1, f], prv)

    def got_f(h, f):
        return remote(block(-h, f), block(-h, f), one_s.at[0], z_r.at[2 * h - 2, f], nxt)

    def got_b(h, f):
        return remote(block(h, f), block(h, f), one_s.at[0], z_r.at[2 * h - 1, f], prv)

    def send_y(off, f):
        return remote(block(off, f), block(off, f), one_s.at[1], agy_r.at[f], yp)

    for f in range(NF):
        send_f(0, f).start()
        send_b(0, f).start()
        send_y(0, f).start()

    def swap(b):
        return remote(p_ref.at[rows(b), :], far_ref.at[rows(b), :], one_s.at[2], px_r.at[b], pp)

    def start_swap(b, _):
        swap(b).start()
        return 0

    lax.fori_loop(0, PB // QB, start_swap, 0)

    def embed_block(b, _):
        e, inv_rms, inv_len = embed(p_ref[rows(b), :])
        for f in range(NF):
            pb[f, rows(b), :] = e[:, f * FC:(f + 1) * FC].astype(BF16)
        pstat[0, rows(b), :] = inv_rms
        pstat[1, rows(b), :] = inv_len
        return 0

    def embed_far(b, _):
        swap(b).wait_recv()
        e, _, _ = embed(far_ref[rows(b), :])
        for f in range(NF):
            pb[f, rows(b + PB // QB), :] = e[:, f * FC:(f + 1) * FC].astype(BF16)
        return 0

    lax.fori_loop(0, PB // QB, embed_block, 0)

    loads[2].wait()
    lane = lax.broadcasted_iota(jnp.int32, (PB, NQ), 1)
    row = lax.broadcasted_iota(jnp.int32, (PB, NQ), 0)
    own = (lane == ci * QB + row // 8).astype(F32)
    ids = lax.broadcasted_iota(jnp.int32, (PB, QB), 0) + dx * PB
    flag = jnp.sum((ids == pos_ref[...]).astype(F32), axis=1, keepdims=True)

    for h in range(1, 5):
        for f in range(NF):
            forth = f < NF // 2
            if h < 4 or forth:
                got_f(h, f).wait_recv()
                if h < 3 or (h == 3 and forth):
                    send_f(h, f).start()
                send_y(-h, f).start()
            if h < 4 or not forth:
                got_b(h, f).wait_recv()
                if h < 3 or (h == 3 and not forth):
                    send_b(h, f).start()
                send_y(h, f).start()
        lax.fori_loop(max(2 * h - 3, 0), 8 if h == 4 else 2 * h - 1, embed_far, 0)

    for f in range(NF):
        arrived = qb.at[f, rows(1 - c, RING * QB), :]
        remote(arrived, arrived, one_s.at[1], agy_r.at[f], yp).wait_recv()
        part = lax.dot_general(pb[f], qb[f], (((1,), (1,)), ((), ())), preferred_element_type=F32)
        sc[...] = part if f == 0 else sc[...] + part
    sc[...] = sc[...] * LOGIT_SCALE

    is_pos = own * flag
    weights = 1.0 + HARD_WEIGHT * (own - is_pos)
    s_own = sc[0:PB, :]
    s_far = sc[PB:NP, :]
    top = jnp.maximum(jnp.max(s_own, axis=0, keepdims=True), jnp.max(s_far, axis=0, keepdims=True))
    e_own = weights * jnp.exp(s_own - top)
    e_far = jnp.exp(s_far - top)
    total = jnp.sum(e_own, axis=0, keepdims=True) + jnp.sum(e_far, axis=0, keepdims=True)
    stats[ci, 0:1, :] = top
    stats[ci, 1:2, :] = total

    def to_class(ref, i):
        for j in (4, 3, 5, 2, 6, 1, 7, 0):
            remote(ref.at[ci], ref.at[ci], one_s.at[i], one_r.at[i], in_class(j, 1 - c)).start()
            if j:
                remote(ref.at[ci], ref.at[ci], one_s.at[i], one_r.at[i], in_class(j, c)).start()

    def several(ref, i, n):
        part = ref.at[pl.ds(0, n)]
        return remote(part, part, one_s.at[i], one_r.at[i], pp)

    to_class(stats, 3)

    offs = (4, 3, -3, 2, -2, 1, -1, 0)
    slot_after = (None, 3, 4, 5, 6, 7, 0)

    def dest(i, cc):
        return rows(cc * RING + (r + offs[i] + RING) % RING)

    et[:, 0:PB] = jnp.transpose(e_own).astype(BF16)
    et[:, PB:NP] = jnp.transpose(e_far).astype(BF16)
    theirs = rows(1 - c, RING * QB)
    for f in range(NF):
        dq[f, theirs, :] = jnp.dot(et[theirs, :], pb[f], preferred_element_type=F32).astype(BF16)

    def send_rsy(i0, i1):
        for i in range(i0, i1):
            for f in range(NF):
                remote(dq.at[f, dest(i, 1 - c), :], yr.at[i, f], one_s.at[4], rsy_r.at[i, f], yp).start()

    send_rsy(0, 3)
    pos_score = jnp.sum(is_pos * s_own, axis=0, keepdims=True)
    several(stats, 3, 15).wait_recv()
    top_all = stats[0, 0:1, :]
    for k in range(1, CLASS):
        top_all = jnp.maximum(top_all, stats[k, 0:1, :])
    sum_all = jnp.zeros((1, NQ), F32)
    for k in range(CLASS):
        sum_all = sum_all + stats[k, 1:2, :] * jnp.exp(stats[k, 0:1, :] - top_all)
    log_total = top_all + jnp.log(sum_all)
    lane1 = lax.broadcasted_iota(jnp.int32, (1, NQ), 1)
    loss_part = jnp.sum(
        jnp.where(lane1 // QB == ci, log_total - pos_score, 0.0), axis=1, keepdims=True
    )

    ds[0:PB, :] = (weights * jnp.exp(s_own - log_total) - is_pos).astype(BF16)
    ds[PB:NP, :] = jnp.exp(s_far - log_total).astype(BF16)
    ds_f = ds[...].astype(F32)
    et[...] = jnp.transpose(ds_f).astype(BF16)
    scale = LOGIT_SCALE * jnp.exp(stats[(1 - c) * RING + r, 0:1, :] - log_total)
    from_y[...] = jnp.transpose(jnp.broadcast_to(scale, (8, NQ)))[:, 0:1]

    rest = pl.ds(FC, D - FC)

    def dp_first():
        return remote(dps.at[:, pl.ds(0, FC)], dpr.at[:, pl.ds(0, FC)], one_s.at[5], one_r.at[5], pp)

    def dp_block(b):
        return remote(dps.at[rows(b), rest], dpr.at[rows(b), rest], one_s.at[5], dp_r.at[b], pp)

    def start_dp(b, _):
        dp_block(b).start()
        return 0

    for f in range(NF):
        d = LOGIT_SCALE * jnp.dot(ds[...], qb[f], preferred_element_type=F32)
        dp[:, f * FC:(f + 1) * FC] = d[0:PB, :]
        dps[:, f * FC:(f + 1) * FC] = d[PB:NP, :].astype(BF16)
        if f == 0:
            dp_first().start()

    ours = rows(c, RING * QB)
    for f in range(NF):
        dq[f, ours, :] = (LOGIT_SCALE * jnp.dot(et[ours, :], pb[f], preferred_element_type=F32)).astype(BF16)

    def zr_got(i, f):
        return remote(zs.at[0, f], zr.at[i, f], one_s.at[6], z_r.at[i, f], nxt)

    def ring_step(i):
        for f in range(NF):
            forth = f < NF // 2
            rsy = remote(yr.at[i, f], yr.at[i, f], one_s.at[4], rsy_r.at[i, f], yp)
            rsy.wait_recv()
            acc = dq[f, dest(i, c), :].astype(F32) + yr[i, f].astype(F32) * from_y[dest(i, c), :]
            if i >= 3 or (i == 1 and forth) or (i == 2 and not forth):
                zr_got(i, f).wait_recv()
                acc = acc + zr[i, f].astype(F32)
            zs[i, f] = acc.astype(BF16)
            ahead = forth if i == 0 else i % 2 == 1
            after = (1 if forth else 2) if i == 0 else slot_after[i]
            remote(zs.at[i, f], zr.at[after, f], one_s.at[6], z_r.at[after, f], nxt if ahead else prv).start()

    ring_step(0)

    prod = ds_f * sc[...]
    u = jnp.sum(prod, axis=1, keepdims=True)
    t_row = jnp.sum(prod, axis=0, keepdims=True)
    t = jnp.transpose(jnp.broadcast_to(t_row, (8, NQ)))[:, 0:1]
    for f in range(NF):
        cols = slice(f * FC, (f + 1) * FC)
        p_own = pb[f, 0:PB, :].astype(F32)
        p_far = pb[f, PB:NP, :].astype(F32)
        q_f = qb[f].astype(F32)
        g = (
            jnp.sum(p_own * (2.0 * dp[:, cols] - p_own * u[0:PB]), axis=0, keepdims=True)
            + jnp.sum(p_far * (2.0 * dps[:, cols].astype(F32) - p_far * u[PB:NP]), axis=0, keepdims=True)
            - jnp.sum(q_f * q_f * t, axis=0, keepdims=True)
        ) / gain_ref[:, cols]
        for k in range(FC // SEG):
            ga[f * (FC // SEG) + k, 0:1, :] = g[:, k * SEG:(k + 1) * SEG]
            ga[f * (FC // SEG) + k, 1:2, :] = jnp.broadcast_to(loss_part, (1, SEG))

    def to_plane(src_of, dst, i):
        def go(k, _):
            remote(src_of((plane + k) % PLANE), dst.at[plane], one_s.at[i], one_r.at[i], *in_plane(k)).start()
            return 0

        lax.fori_loop(1, PLANE, go, 0)

    to_plane(lambda other: ga.at[other], gar, 7)
    gar[plane] = ga[plane]
    lax.fori_loop(0, 4, start_dp, 0)
    send_rsy(3, 5)
    ring_step(1)
    ring_step(2)
    send_rsy(5, 8)
    lax.fori_loop(4, PB // QB, start_dp, 0)

    several(gar, 7, PLANE - 1).wait_recv()
    seg = gar[0]
    for k in range(1, PLANE):
        seg = seg + gar[k]
    gc[tall] = seg

    def over_z(k, _):
        remote(gc.at[tall], gc.at[tall], one_s.at[9], one_r.at[9], *along_z(k)).start()
        return 0

    lax.fori_loop(1, 16, over_z, 0)

    def backward(hidden, inv_rms, inv_len, d):
        g = gain_ref[...]
        unit = hidden.astype(F32) * inv_rms
        e = unit * g * inv_len
        dnormed = inv_len * (d - e * jnp.sum(e * d, axis=1, keepdims=True))
        dunit = dnormed * g
        mean = jnp.sum(dunit * unit, axis=1, keepdims=True) * (1.0 / D)
        return (inv_rms * (dunit - unit * mean)).astype(BF16)

    def p_block(b, _):
        dp_block(b).wait_recv()
        at = rows(b)
        d = dp[at, :] + dpr[at, :].astype(F32)
        pg_ref[at, :] = backward(p_ref[at, :], pstat[0, at, :], pstat[1, at, :], d)
        return 0

    def p_blocks(b0, b1):
        lax.fori_loop(b0, b1, p_block, 0)

    ring_step(3)
    ring_step(4)
    dp_first().wait_recv()
    p_blocks(0, 2)
    ring_step(5)
    ring_step(6)

    several(gc, 9, 15).wait_recv()
    seg = gc[0]
    for k in range(1, 16):
        seg = seg + gc[k]
    gd[plane] = seg
    to_plane(lambda other: gd.at[plane], gd, 10)
    p_blocks(2, 6)

    for f in range(NF):
        rsy = remote(yr.at[RING - 1, f], yr.at[RING - 1, f], one_s.at[4], rsy_r.at[RING - 1, f], yp)
        rsy.wait_recv()
        zr_got(7, f).wait_recv()
        zr_got(0, f).wait_recv()
        dfin[:, f * FC:(f + 1) * FC] = (
            dq[f, dest(7, c), :].astype(F32) + yr[RING - 1, f].astype(F32) * from_y[dest(7, c), :]
            + (zr[7, f].astype(F32) + zr[0, f].astype(F32))
        )
    _, q_rms, q_len = embed(q_ref[...])
    qg_ref[...] = backward(q_ref[...], q_rms, q_len, dfin[...])
    p_blocks(6, 8)

    several(gd, 10, PLANE - 1).wait_recv()
    for k in range(PLANE):
        gg_ref[:, k * SEG:(k + 1) * SEG] = gd[k, 0:1, :]
    loss_ref[...] = gd[0, 1:2, 0:1]

    for ref, i in (
        (qb.at[:, pl.ds(0, 7 * QB), :], 0), (qb.at[:, pl.ds(0, 8 * QB), :], 1), (far_ref, 2),
        (yr, 4), (dpr, 5), (zs.at[pl.ds(0, 7)], 6),
    ):
        remote(ref, ref, one_s.at[i], one_r.at[i], pp).wait_send()
    for ref, i, n in ((stats, 3, 15), (gar, 7, PLANE - 1), (gc, 9, 15), (gd, 10, PLANE - 1)):
        several(ref, i, n).wait_send()


def on_device(query_hidden, passage_hidden, gain, hard_ids, positive_ids):
    del hard_ids
    vmem = pl.BlockSpec(memory_space=pltpu.VMEM)
    hbm = pl.BlockSpec(memory_space=pltpu.HBM)
    dma = pltpu.SemaphoreType.DMA
    query_grad, passage_grad, gain_grad, loss = pl.pallas_call(
        kernel,
        out_shape=(
            jax.ShapeDtypeStruct((QB, D), BF16),
            jax.ShapeDtypeStruct((PB, D), BF16),
            jax.ShapeDtypeStruct((1, D), F32),
            jax.ShapeDtypeStruct((1, 1), F32),
        ),
        in_specs=[hbm] * 4,
        out_specs=(vmem,) * 4,
        scratch_shapes=[
            pltpu.VMEM((QB, D), BF16),
            pltpu.VMEM((PB, D), BF16),
            pltpu.VMEM((PB, D), BF16),
            pltpu.VMEM((1, D), F32),
            pltpu.VMEM((1, QB), jnp.int32),
            pltpu.VMEM((NF, NQ, FC), BF16),
            pltpu.VMEM((NF, NP, FC), BF16),
            pltpu.VMEM((NP, NQ), F32),
            pltpu.VMEM((NP, NQ), BF16),
            pltpu.VMEM((NF, NQ, FC), BF16),
            pltpu.VMEM((RING, NF, QB, FC), BF16),
            pltpu.VMEM((RING, NF, QB, FC), BF16),
            pltpu.VMEM((RING, NF, QB, FC), BF16),
            pltpu.VMEM((PB, D), F32),
            pltpu.VMEM((PB, D), BF16),
            pltpu.VMEM((PB, D), BF16),
            pltpu.VMEM((QB, D), F32),
            pltpu.VMEM((2, PB, 1), F32),
            pltpu.VMEM((CLASS, 2, NQ), F32),
            pltpu.VMEM((PLANE, 2, SEG), F32),
            pltpu.VMEM((PLANE, 2, SEG), F32),
            pltpu.VMEM((16, 2, SEG), F32),
            pltpu.VMEM((PLANE, 2, SEG), F32),
            pltpu.VMEM((NQ, NP), BF16),
            pltpu.VMEM((NQ, 1), F32),
            dma((4,)),
            dma((RING, NF)),
            dma((RING, NF)),
            dma((PB // QB,)),
            dma((PB // QB,)),
            dma((NF,)),
            dma((11,)),
            dma((11,)),
        ],
        compiler_params=pltpu.CompilerParams(
            collective_id=0, has_side_effects=True, vmem_limit_bytes=60 * 1024 * 1024
        ),
        cost_estimate=pl.CostEstimate(flops=1_610_612_736, bytes_accessed=2_400_000, transcendentals=200_000),
    )(query_hidden, passage_hidden, gain.reshape(1, D), positive_ids.reshape(1, QB))
    return query_grad, passage_grad, gain_grad.reshape(D), loss.reshape(())


def solution(mesh):
    placed = (
        P(("dx", "dy"), None),
        P(("dx", "dy"), None),
        P(),
        P(("dx", "dy"), None),
        P(("dx", "dy")),
    )
    return jax.shard_map(
        on_device,
        mesh=mesh,
        in_specs=placed,
        out_specs=(P(("dx", "dy"), None), P(("dx", "dy"), None), P(), P()),
        check_vma=False,
    )
```

```python
import jax
import jax.numpy as jnp
from jax import lax
from jax.experimental import pallas as pl
from jax.experimental.pallas import tpu as pltpu
from jax.sharding import PartitionSpec as P

MESH = pl.DeviceIdType.MESH
F32 = jnp.float32
BF16 = jnp.bfloat16

LOGIT_SCALE = 250.0
HARD_WEIGHT = 3.0
D = 4096
QB = 16
PB = 128
RING = 8
CLASS = 16
NQ = QB * CLASS
NP = 2 * PB
NF = 4
FC = D // NF
SIDE = 8
SEG = D // SIDE
SUB = SEG // 4


def kernel(
    q_hbm, p_hbm, gain_hbm, pos_hbm,
    qg_ref, pg_ref, gg_ref, loss_ref,
    q_ref, p_ref, far_ref, gain_ref, pos_ref,
    qb, pb, sc, ds, dq, yr, zs, zr, dp, dps, dpr, dfin, pstat, stats, ga, gar, gy, gyr, gc, gd, ge, et, from_y, qg_v, pg_v, gg_v, loss_v,
    in_sem, z_r, rsy_r, dp_r, px_r, agy_r, one_s, one_r,
):
    dx = lax.axis_index("dx")
    dy = lax.axis_index("dy")
    y = dx & 3
    z = dx >> 2
    half = z >> 1
    r = half + (z & 1) * (7 - 2 * half)
    c = y >> 1
    cls = (y + c) & 1
    ci = c * RING + r

    def z_of(place):
        return 2 * place + (place >> 2) * (15 - 4 * place)

    nxt = z_of((r + 1) & 7) * 4 + y
    prv = z_of((r + 7) & 7) * 4 + y
    yp = z * 4 + 3 - y
    pp = z * 4 + y + 1 - 2 * (y & 1)

    x = dy >> 2
    z_hi = (dy >> 1) & 1
    core = dy & 1
    side = x * 2 + core
    tall = z_hi * RING + z

    def along_side(k):
        other = (side + k) & 7
        return dx, (other >> 1) * 4 + z_hi * 2 + (other & 1)

    def along_y(k):
        return z * 4 + ((y + k) & 3), dy

    def along_z(k):
        other = (tall + k) & 15
        return (other & 7) * 4 + y, x * 4 + (other >> 3) * 2 + core

    def in_class(j, cc):
        return z_of((r + j) & 7) * 4 + cls + cc * (3 - 2 * cls)

    def rows(block, size=QB):
        return pl.ds(pl.multiple_of(block * size, size), size)

    def remote(src, dst, send, recv, dev, other_dy=None):
        return pltpu.make_async_remote_copy(
            src_ref=src, dst_ref=dst, send_sem=send, recv_sem=recv,
            device_id=(dev, dy if other_dy is None else other_dy), device_id_type=MESH,
        )

    loads = [
        pltpu.make_async_copy(src, dst, in_sem.at[i])
        for i, (src, dst) in enumerate(
            ((q_hbm, q_ref), (gain_hbm, gain_ref), (pos_hbm, pos_ref), (p_hbm, p_ref))
        )
    ]
    for load in loads:
        load.start()

    barrier = pltpu.get_barrier_semaphore()

    def greet(dev, other_dy):
        pl.semaphore_signal(barrier, inc=1, device_id=(dev, other_dy), device_id_type=MESH)

    for k in range(1, 4):
        greet(*along_y(k))
    for k in range(1, RING):
        greet(in_class(k, 1 - c), dy)
    for k in (8, 7, 9, 6, 10, 5, 11, 4, 12, 3, 13, 2, 14, 1, 15):
        greet(*along_z(k))
    for k in range(1, SIDE):
        greet(*along_side(k))

    def embed(hidden):
        v = hidden.astype(F32)
        vg = v * gain_ref[...]
        inv_rms = lax.rsqrt(jnp.sum(v * v, axis=1, keepdims=True) * (1.0 / D) + 1e-05)
        inv_len = lax.rsqrt(jnp.sum(vg * vg, axis=1, keepdims=True) * (inv_rms * inv_rms) + 1e-06)
        return vg * (inv_rms * inv_len), inv_rms, inv_len

    loads[0].wait()
    loads[1].wait()
    q_e, _, _ = embed(q_ref[...])
    for f in range(NF):
        qb[f, rows(ci), :] = q_e[:, f * FC:(f + 1) * FC].astype(BF16)

    loads[3].wait()
    pl.semaphore_wait(barrier, 3 + 7 + 15 + 7)

    def block(off, f, cc=None):
        return qb.at[f, rows((c if cc is None else cc) * RING + ((r + off) & 7)), :]

    def send_f(h, f):
        return remote(block(-h, f), block(-h, f), one_s.at[0], z_r.at[2 * h, f], nxt)

    def send_b(h, f):
        return remote(block(h, f), block(h, f), one_s.at[0], z_r.at[2 * h + 1, f], prv)

    def got_f(h, f):
        return remote(block(-h, f), block(-h, f), one_s.at[0], z_r.at[2 * h - 2, f], nxt)

    def got_b(h, f):
        return remote(block(h, f), block(h, f), one_s.at[0], z_r.at[2 * h - 1, f], prv)

    def send_y(off, f):
        return remote(block(off, f), block(off, f), one_s.at[1], agy_r.at[f], yp)

    def swap(b):
        return remote(p_ref.at[rows(b), :], far_ref.at[rows(b), :], one_s.at[2], px_r.at[b], pp)

    swap(0).start()
    swap(1).start()
    for f in range(NF):
        send_f(0, f).start()
        send_b(0, f).start()
        send_y(0, f).start()
    for b in range(2, PB // QB):
        swap(b).start()

    def embed_block(b, _):
        e, inv_rms, inv_len = embed(p_ref[rows(b), :])
        for f in range(NF):
            pb[f, rows(b), :] = e[:, f * FC:(f + 1) * FC].astype(BF16)
        pstat[0, rows(b), :] = inv_rms
        pstat[1, rows(b), :] = inv_len
        return 0

    def embed_far(b, _):
        swap(b).wait_recv()
        e, _, _ = embed(far_ref[rows(b), :])
        for f in range(NF):
            pb[f, rows(b + PB // QB), :] = e[:, f * FC:(f + 1) * FC].astype(BF16)
        return 0

    lax.fori_loop(0, PB // QB, embed_block, 0)

    loads[2].wait()
    lane = lax.broadcasted_iota(jnp.int32, (PB, NQ), 1)
    row = lax.broadcasted_iota(jnp.int32, (PB, NQ), 0)
    own = (lane == ci * QB + row // 8).astype(F32)
    ids = lax.broadcasted_iota(jnp.int32, (PB, QB), 0) + dx * PB
    flag = jnp.sum((ids == pos_ref[...]).astype(F32), axis=1, keepdims=True)

    for h in range(1, 5):
        for f in range(NF):
            forth = f < NF // 2
            if h < 4 or forth:
                got_f(h, f).wait_recv()
                if h < 3 or (h == 3 and forth):
                    send_f(h, f).start()
                send_y(-h, f).start()
            if h < 4 or not forth:
                got_b(h, f).wait_recv()
                if h < 3 or (h == 3 and not forth):
                    send_b(h, f).start()
                send_y(h, f).start()
        lax.fori_loop(max(2 * h - 3, 0), 8 if h == 4 else 2 * h - 1, embed_far, 0)

    for f in range(NF):
        arrived = qb.at[f, rows(1 - c, RING * QB), :]
        remote(arrived, arrived, one_s.at[1], agy_r.at[f], yp).wait_recv()
        part = lax.dot_general(pb[f], qb[f], (((1,), (1,)), ((), ())), preferred_element_type=F32)
        sc[...] = part if f == 0 else sc[...] + part
    sc[...] = sc[...] * LOGIT_SCALE

    is_pos = own * flag
    weights = 1.0 + HARD_WEIGHT * (own - is_pos)
    s_own = sc[0:PB, :]
    s_far = sc[PB:NP, :]
    top = jnp.maximum(jnp.max(s_own, axis=0, keepdims=True), jnp.max(s_far, axis=0, keepdims=True))
    e_own = weights * jnp.exp(s_own - top)
    e_far = jnp.exp(s_far - top)
    total = jnp.sum(e_own, axis=0, keepdims=True) + jnp.sum(e_far, axis=0, keepdims=True)
    stats[ci, 0:1, :] = top
    stats[ci, 1:2, :] = total

    def to_class(ref, i):
        for j in (4, 3, 5, 2, 6, 1, 7, 0):
            remote(ref.at[ci], ref.at[ci], one_s.at[i], one_r.at[i], in_class(j, 1 - c)).start()
            if j:
                remote(ref.at[ci], ref.at[ci], one_s.at[i], one_r.at[i], in_class(j, c)).start()

    def several(ref, i, n):
        part = ref.at[pl.ds(0, n)]
        return remote(part, part, one_s.at[i], one_r.at[i], pp)

    to_class(stats, 3)

    offs = (4, 3, -3, 2, -2, 1, -1, 0)
    slot_after = (None, 3, 4, 5, 6, 7, 0)

    def dest(i, cc):
        return rows(cc * RING + ((r + offs[i]) & 7))

    et[:, 0:PB] = jnp.transpose(e_own).astype(BF16)
    et[:, PB:NP] = jnp.transpose(e_far).astype(BF16)
    theirs = rows(1 - c, RING * QB)
    for f in range(NF):
        dq[f, theirs, :] = jnp.dot(et[theirs, :], pb[f], preferred_element_type=F32).astype(BF16)

    def send_rsy(i0, i1):
        for i in range(i0, i1):
            for f in range(NF):
                remote(dq.at[f, dest(i, 1 - c), :], yr.at[i, f], one_s.at[4], rsy_r.at[i, f], yp).start()

    send_rsy(0, 3)
    pos_score = jnp.sum(is_pos * s_own, axis=0, keepdims=True)
    several(stats, 3, 15).wait_recv()
    top_all = stats[0, 0:1, :]
    for k in range(1, CLASS):
        top_all = jnp.maximum(top_all, stats[k, 0:1, :])
    sum_all = jnp.zeros((1, NQ), F32)
    for k in range(CLASS):
        sum_all = sum_all + stats[k, 1:2, :] * jnp.exp(stats[k, 0:1, :] - top_all)
    log_total = top_all + jnp.log(sum_all)
    lane1 = lax.broadcasted_iota(jnp.int32, (1, NQ), 1)
    loss_part = jnp.sum(
        jnp.where(lane1 // QB == ci, log_total - pos_score, 0.0), axis=1, keepdims=True
    )

    ds[0:PB, :] = (weights * jnp.exp(s_own - log_total) - is_pos).astype(BF16)
    ds[PB:NP, :] = jnp.exp(s_far - log_total).astype(BF16)
    ds_f = ds[...].astype(F32)
    rest = pl.ds(FC, D - FC)

    def dp_first():
        return remote(dps.at[:, pl.ds(0, FC)], dpr.at[:, pl.ds(0, FC)], one_s.at[5], one_r.at[5], pp)

    def dp_block(b):
        return remote(dps.at[rows(b), rest], dpr.at[rows(b), rest], one_s.at[5], dp_r.at[b], pp)

    def start_dp(b, _):
        dp_block(b).start()
        return 0

    for f in range(NF):
        d = LOGIT_SCALE * jnp.dot(ds[...], qb[f], preferred_element_type=F32)
        dp[:, f * FC:(f + 1) * FC] = d[0:PB, :]
        dps[:, f * FC:(f + 1) * FC] = d[PB:NP, :].astype(BF16)
        if f == 0:
            dp_first().start()

    et[...] = jnp.transpose(ds_f).astype(BF16)
    scale = LOGIT_SCALE * jnp.exp(stats[(1 - c) * RING + r, 0:1, :] - log_total)
    from_y[...] = jnp.transpose(jnp.broadcast_to(scale, (8, NQ)))[:, 0:1]
    ours = rows(c, RING * QB)
    for f in range(NF):
        dq[f, ours, :] = (LOGIT_SCALE * jnp.dot(et[ours, :], pb[f], preferred_element_type=F32)).astype(BF16)

    def zr_got(i, f):
        return remote(zs.at[0, f], zr.at[i, f], one_s.at[6], z_r.at[i, f], nxt)

    def ring_step(i):
        for f in range(NF):
            forth = f < NF // 2
            rsy = remote(yr.at[i, f], yr.at[i, f], one_s.at[4], rsy_r.at[i, f], yp)
            rsy.wait_recv()
            acc = dq[f, dest(i, c), :].astype(F32) + yr[i, f].astype(F32) * from_y[dest(i, c), :]
            if i >= 3 or (i == 1 and forth) or (i == 2 and not forth):
                zr_got(i, f).wait_recv()
                acc = acc + zr[i, f].astype(F32)
            zs[i, f] = acc.astype(BF16)
            ahead = forth if i == 0 else i % 2 == 1
            after = (1 if forth else 2) if i == 0 else slot_after[i]
            remote(zs.at[i, f], zr.at[after, f], one_s.at[6], z_r.at[after, f], nxt if ahead else prv).start()

    ring_step(0)

    prod = ds_f * sc[...]
    u = jnp.sum(prod, axis=1, keepdims=True)
    t_row = jnp.sum(prod, axis=0, keepdims=True)
    t = jnp.transpose(jnp.broadcast_to(t_row, (8, NQ)))[:, 0:1]
    for f in range(NF):
        cols = slice(f * FC, (f + 1) * FC)
        p_own = pb[f, 0:PB, :].astype(F32)
        p_far = pb[f, PB:NP, :].astype(F32)
        q_f = qb[f].astype(F32)
        g = (
            jnp.sum(p_own * (2.0 * dp[:, cols] - p_own * u[0:PB]), axis=0, keepdims=True)
            + jnp.sum(p_far * (2.0 * dps[:, cols].astype(F32) - p_far * u[PB:NP]), axis=0, keepdims=True)
            - jnp.sum(q_f * q_f * t, axis=0, keepdims=True)
        ) / gain_ref[:, cols]
        for k in range(FC // SEG):
            ga[f * (FC // SEG) + k, 0:1, :] = g[:, k * SEG:(k + 1) * SEG]
            ga[f * (FC // SEG) + k, 1:2, :] = jnp.broadcast_to(loss_part, (1, SEG))

    def spread(n, to, src_of, dst, i, order=None):
        for k in order or range(1, n):
            dev, other_dy = to(k)
            remote(src_of(k), dst, one_s.at[i], one_r.at[i], dev, other_dy).start()

    def total_of(ref, n):
        out = ref[0]
        for k in range(1, n):
            out = out + ref[k]
        return out

    spread(SIDE, along_side, lambda k: ga.at[(side + k) & 7], gar.at[side], 7)
    gar[side] = ga[side]
    lax.fori_loop(0, 4, start_dp, 0)
    send_rsy(3, 5)
    ring_step(1)
    several(gar, 7, SIDE - 1).wait_recv()
    seg = total_of(gar, SIDE)
    for k in range(4):
        gy[k] = seg[:, k * SUB:(k + 1) * SUB]
    spread(4, along_y, lambda k: gy.at[(y + k) & 3], gyr.at[y], 8)
    gyr[y] = gy[y]
    ring_step(2)
    send_rsy(5, 8)
    lax.fori_loop(4, PB // QB, start_dp, 0)

    several(gyr, 8, 3).wait_recv()
    gc[tall] = total_of(gyr, 4)
    spread(16, along_z, lambda k: gc.at[tall], gc.at[tall], 9, (8, 7, 9, 6, 10, 5, 11, 4, 12, 3, 13, 2, 14, 1, 15))

    def backward(hidden, inv_rms, inv_len, d):
        g = gain_ref[...]
        unit = hidden.astype(F32) * inv_rms
        e = unit * g * inv_len
        dnormed = inv_len * (d - e * jnp.sum(e * d, axis=1, keepdims=True))
        dunit = dnormed * g
        mean = jnp.sum(dunit * unit, axis=1, keepdims=True) * (1.0 / D)
        return (inv_rms * (dunit - unit * mean)).astype(BF16)

    def p_block(b, _):
        dp_block(b).wait_recv()
        at = rows(b)
        d = dp[at, :] + dpr[at, :].astype(F32)
        pg_v[at, :] = backward(p_ref[at, :], pstat[0, at, :], pstat[1, at, :], d)
        pltpu.make_async_copy(pg_v.at[at, :], pg_ref.at[at, :], in_sem.at[3]).start()
        return 0

    def p_blocks(b0, b1):
        lax.fori_loop(b0, b1, p_block, 0)

    ring_step(3)
    ring_step(4)
    dp_first().wait_recv()
    p_blocks(0, 2)
    several(gc, 9, 15).wait_recv()
    gd[y] = total_of(gc, 16)
    spread(4, along_y, lambda k: gd.at[y], gd.at[y], 10)
    ring_step(5)
    ring_step(6)
    several(gd, 10, 3).wait_recv()
    for k in range(4):
        ge[side, :, k * SUB:(k + 1) * SUB] = gd[k]
    spread(SIDE, along_side, lambda k: ge.at[side], ge.at[side], 11)
    p_blocks(2, 6)

    for f in range(NF):
        rsy = remote(yr.at[RING - 1, f], yr.at[RING - 1, f], one_s.at[4], rsy_r.at[RING - 1, f], yp)
        rsy.wait_recv()
        zr_got(7, f).wait_recv()
        zr_got(0, f).wait_recv()
        dfin[:, f * FC:(f + 1) * FC] = (
            dq[f, dest(7, c), :].astype(F32) + yr[RING - 1, f].astype(F32) * from_y[dest(7, c), :]
            + (zr[7, f].astype(F32) + zr[0, f].astype(F32))
        )
    _, q_rms, q_len = embed(q_ref[...])
    qg_v[...] = backward(q_ref[...], q_rms, q_len, dfin[...])
    p_blocks(6, 8)

    several(ge, 11, SIDE - 1).wait_recv()
    for k in range(SIDE):
        gg_v[:, k * SEG:(k + 1) * SEG] = ge[k, 0:1, :]
    loss_v[...] = ge[0, 1:2, 0:1]
    stores = [
        pltpu.make_async_copy(src, dst, in_sem.at[i])
        for i, (src, dst) in enumerate(((qg_v, qg_ref), (gg_v, gg_ref), (loss_v, loss_ref)))
    ]
    for store in stores:
        store.start()
    for store in stores:
        store.wait()
    pltpu.make_async_copy(pg_v, pg_ref, in_sem.at[3]).wait()

    for ref, i in (
        (qb.at[:, pl.ds(0, 7 * QB), :], 0), (qb.at[:, pl.ds(0, 8 * QB), :], 1), (far_ref, 2),
        (yr, 4), (dpr, 5), (zs.at[pl.ds(0, 7)], 6),
    ):
        remote(ref, ref, one_s.at[i], one_r.at[i], pp).wait_send()
    for ref, i, n in (
        (stats, 3, 15), (gar, 7, SIDE - 1), (gyr, 8, 3), (gc, 9, 15), (gd, 10, 3), (ge, 11, SIDE - 1)
    ):
        several(ref, i, n).wait_send()


def hand_over(qg_in, pg_in, gg_in, qg_ref, pg_ref, gg_ref, sems):
    part = PB // 4
    copies = [pltpu.make_async_copy(qg_in, qg_ref, sems.at[0]), pltpu.make_async_copy(gg_in, gg_ref, sems.at[1])]
    for i in range(4):
        at = pl.ds(i * part, part)
        copies.append(pltpu.make_async_copy(pg_in.at[at, :], pg_ref.at[at, :], sems.at[2 + i]))
    for copy in copies:
        copy.start()
    for copy in copies:
        copy.wait()


def on_device(query_hidden, passage_hidden, gain, hard_ids, positive_ids):
    del hard_ids
    hbm = pl.BlockSpec(memory_space=pltpu.HBM)
    any_space = pl.BlockSpec(memory_space=pl.ANY)
    dma = pltpu.SemaphoreType.DMA
    shapes = (
        jax.ShapeDtypeStruct((QB, D), BF16),
        jax.ShapeDtypeStruct((PB, D), BF16),
        jax.ShapeDtypeStruct((1, D), F32),
    )
    query_grad, passage_grad, gain_grad, loss = pl.pallas_call(
        kernel,
        out_shape=(*shapes, jax.ShapeDtypeStruct((1, 1), F32)),
        in_specs=[hbm] * 4,
        out_specs=(any_space,) * 4,
        scratch_shapes=[
            pltpu.VMEM((QB, D), BF16),
            pltpu.VMEM((PB, D), BF16),
            pltpu.VMEM((PB, D), BF16),
            pltpu.VMEM((1, D), F32),
            pltpu.VMEM((1, QB), jnp.int32),
            pltpu.VMEM((NF, NQ, FC), BF16),
            pltpu.VMEM((NF, NP, FC), BF16),
            pltpu.VMEM((NP, NQ), F32),
            pltpu.VMEM((NP, NQ), BF16),
            pltpu.VMEM((NF, NQ, FC), BF16),
            pltpu.VMEM((RING, NF, QB, FC), BF16),
            pltpu.VMEM((RING, NF, QB, FC), BF16),
            pltpu.VMEM((RING, NF, QB, FC), BF16),
            pltpu.VMEM((PB, D), F32),
            pltpu.VMEM((PB, D), BF16),
            pltpu.VMEM((PB, D), BF16),
            pltpu.VMEM((QB, D), F32),
            pltpu.VMEM((2, PB, 1), F32),
            pltpu.VMEM((CLASS, 2, NQ), F32),
            pltpu.VMEM((SIDE, 2, SEG), F32),
            pltpu.VMEM((SIDE, 2, SEG), F32),
            pltpu.VMEM((4, 2, SUB), F32),
            pltpu.VMEM((4, 2, SUB), F32),
            pltpu.VMEM((16, 2, SUB), F32),
            pltpu.VMEM((4, 2, SUB), F32),
            pltpu.VMEM((SIDE, 2, SEG), F32),
            pltpu.VMEM((NQ, NP), BF16),
            pltpu.VMEM((NQ, 1), F32),
            pltpu.VMEM((QB, D), BF16),
            pltpu.VMEM((PB, D), BF16),
            pltpu.VMEM((1, D), F32),
            pltpu.VMEM((1, 1), F32),
            dma((4,)),
            dma((RING, NF)),
            dma((RING, NF)),
            dma((PB // QB,)),
            dma((PB // QB,)),
            dma((NF,)),
            dma((12,)),
            dma((12,)),
        ],
        compiler_params=pltpu.CompilerParams(
            collective_id=0, has_side_effects=True, vmem_limit_bytes=60 * 1024 * 1024
        ),
        cost_estimate=pl.CostEstimate(flops=1_610_612_736, bytes_accessed=2_400_000, transcendentals=200_000),
    )(query_hidden, passage_hidden, gain.reshape(1, D), positive_ids.reshape(1, QB))
    query_grad, passage_grad, gain_grad = pl.pallas_call(
        hand_over,
        out_shape=shapes,
        in_specs=[any_space] * 3,
        out_specs=(any_space,) * 3,
        scratch_shapes=[dma((6,))],
        compiler_params=pltpu.CompilerParams(vmem_limit_bytes=60 * 1024 * 1024),
    )(query_grad, passage_grad, gain_grad)
    return query_grad, passage_grad, gain_grad.reshape(D), loss.reshape(())


def solution(mesh):
    placed = (
        P(("dx", "dy"), None),
        P(("dx", "dy"), None),
        P(),
        P(("dx", "dy"), None),
        P(("dx", "dy")),
    )
    return jax.shard_map(
        on_device,
        mesh=mesh,
        in_specs=placed,
        out_specs=(P(("dx", "dy"), None), P(("dx", "dy"), None), P(), P()),
        check_vma=False,
    )
```

```python
import jax
import jax.numpy as jnp
from jax import lax
from jax.experimental import pallas as pl
from jax.experimental.pallas import tpu as pltpu
from jax.sharding import PartitionSpec as P

MESH = pl.DeviceIdType.MESH
F32 = jnp.float32
BF16 = jnp.bfloat16

LOGIT_SCALE = 250.0
HARD_WEIGHT = 3.0
D = 4096
QB = 16
PB = 128
RING = 8
CLASS = 16
NQ = QB * CLASS
NP = 2 * PB
NF = 4
FC = D // NF
PLANE = 32
SEG = D // PLANE


def kernel(
    q_hbm, p_hbm, gain_hbm, pos_hbm,
    qg_ref, pg_ref, gg_ref, loss_ref,
    q_ref, p_ref, far_ref, gain_ref, pos_ref,
    qb, pb, sc, ds, dq, yr, zs, zr, dp, dps, dpr, dfin, pstat, stats, ga, gar, gc, gd, et, from_y, qg_v, pg_v, gg_v, loss_v,
    in_sem, z_r, rsy_r, dp_r, px_r, agy_r, one_s, one_r,
):
    dx = lax.axis_index("dx")
    dy = lax.axis_index("dy")
    y = dx & 3
    z = dx >> 2
    half = z >> 1
    r = half + (z & 1) * (7 - 2 * half)
    c = y >> 1
    cls = (y + c) & 1
    ci = c * RING + r

    def z_of(place):
        return 2 * place + (place >> 2) * (15 - 4 * place)

    nxt = z_of((r + 1) & 7) * 4 + y
    prv = z_of((r + 7) & 7) * 4 + y
    yp = z * 4 + 3 - y
    pp = z * 4 + y + 1 - 2 * (y & 1)

    x = dy >> 2
    z_hi = (dy >> 1) & 1
    core = dy & 1
    plane = (x * 2 + core) * 4 + y
    tall = z_hi * RING + z

    def in_plane(k):
        other = (plane + k) & 31
        return z * 4 + (other & 3), (other >> 3) * 4 + z_hi * 2 + ((other >> 2) & 1)

    def along_z(k):
        other = (tall + k) & 15
        return (other & 7) * 4 + y, x * 4 + (other >> 3) * 2 + core

    def in_class(j, cc):
        return z_of((r + j) & 7) * 4 + cls + cc * (3 - 2 * cls)

    def rows(block, size=QB):
        return pl.ds(pl.multiple_of(block * size, size), size)

    def remote(src, dst, send, recv, dev, other_dy=None):
        return pltpu.make_async_remote_copy(
            src_ref=src, dst_ref=dst, send_sem=send, recv_sem=recv,
            device_id=(dev, dy if other_dy is None else other_dy), device_id_type=MESH,
        )

    loads = [
        pltpu.make_async_copy(src, dst, in_sem.at[i])
        for i, (src, dst) in enumerate(
            ((q_hbm, q_ref), (gain_hbm, gain_ref), (pos_hbm, pos_ref), (p_hbm, p_ref))
        )
    ]
    for load in loads:
        load.start()

    barrier = pltpu.get_barrier_semaphore()

    def greet(dev, other_dy):
        pl.semaphore_signal(barrier, inc=1, device_id=(dev, other_dy), device_id_type=MESH)

    for k in range(1, RING):
        greet(in_class(k, 1 - c), dy)
    for k in (8, 7, 9, 6, 10, 5, 11, 4, 12, 3, 13, 2, 14, 1, 15):
        greet(*along_z(k))
    for k in range(1, PLANE):
        greet(*in_plane(k))

    def embed(hidden):
        v = hidden.astype(F32)
        vg = v * gain_ref[...]
        inv_rms = lax.rsqrt(jnp.sum(v * v, axis=1, keepdims=True) * (1.0 / D) + 1e-05)
        inv_len = lax.rsqrt(jnp.sum(vg * vg, axis=1, keepdims=True) * (inv_rms * inv_rms) + 1e-06)
        return vg * (inv_rms * inv_len), inv_rms, inv_len

    loads[0].wait()
    loads[1].wait()
    q_e, _, _ = embed(q_ref[...])
    for f in range(NF):
        qb[f, rows(ci), :] = q_e[:, f * FC:(f + 1) * FC].astype(BF16)

    loads[3].wait()
    pl.semaphore_wait(barrier, 7 + 15 + 31)

    def block(off, f, cc=None):
        return qb.at[f, rows((c if cc is None else cc) * RING + ((r + off) & 7)), :]

    def send_f(h, f):
        return remote(block(-h, f), block(-h, f), one_s.at[0], z_r.at[2 * h, f], nxt)

    def send_b(h, f):
        return remote(block(h, f), block(h, f), one_s.at[0], z_r.at[2 * h + 1, f], prv)

    def got_f(h, f):
        return remote(block(-h, f), block(-h, f), one_s.at[0], z_r.at[2 * h - 2, f], nxt)

    def got_b(h, f):
        return remote(block(h, f), block(h, f), one_s.at[0], z_r.at[2 * h - 1, f], prv)

    def send_y(off, f):
        return remote(block(off, f), block(off, f), one_s.at[1], agy_r.at[f], yp)

    def swap(b):
        return remote(p_ref.at[rows(b), :], far_ref.at[rows(b), :], one_s.at[2], px_r.at[b], pp)

    swap(0).start()
    swap(1).start()
    for f in range(NF):
        send_f(0, f).start()
        send_b(0, f).start()
        send_y(0, f).start()
    for b in range(2, PB // QB):
        swap(b).start()

    def embed_block(b, _):
        e, inv_rms, inv_len = embed(p_ref[rows(b), :])
        for f in range(NF):
            pb[f, rows(b), :] = e[:, f * FC:(f + 1) * FC].astype(BF16)
        pstat[0, rows(b), :] = inv_rms
        pstat[1, rows(b), :] = inv_len
        return 0

    def embed_far(b, _):
        swap(b).wait_recv()
        e, _, _ = embed(far_ref[rows(b), :])
        for f in range(NF):
            pb[f, rows(b + PB // QB), :] = e[:, f * FC:(f + 1) * FC].astype(BF16)
        return 0

    lax.fori_loop(0, PB // QB, embed_block, 0)

    loads[2].wait()
    lane = lax.broadcasted_iota(jnp.int32, (PB, NQ), 1)
    row = lax.broadcasted_iota(jnp.int32, (PB, NQ), 0)
    own = (lane == ci * QB + row // 8).astype(F32)
    ids = lax.broadcasted_iota(jnp.int32, (PB, QB), 0) + dx * PB
    flag = jnp.sum((ids == pos_ref[...]).astype(F32), axis=1, keepdims=True)

    for h in range(1, 5):
        for f in range(NF):
            forth = f < NF // 2
            if h < 4 or forth:
                got_f(h, f).wait_recv()
                if h < 3 or (h == 3 and forth):
                    send_f(h, f).start()
                send_y(-h, f).start()
            if h < 4 or not forth:
                got_b(h, f).wait_recv()
                if h < 3 or (h == 3 and not forth):
                    send_b(h, f).start()
                send_y(h, f).start()
        lax.fori_loop(max(2 * h - 3, 0), 8 if h == 4 else 2 * h - 1, embed_far, 0)

    for f in range(NF):
        arrived = qb.at[f, rows(1 - c, RING * QB), :]
        remote(arrived, arrived, one_s.at[1], agy_r.at[f], yp).wait_recv()
        part = lax.dot_general(pb[f], qb[f], (((1,), (1,)), ((), ())), preferred_element_type=F32)
        sc[...] = part if f == 0 else sc[...] + part
    sc[...] = sc[...] * LOGIT_SCALE

    is_pos = own * flag
    weights = 1.0 + HARD_WEIGHT * (own - is_pos)
    s_own = sc[0:PB, :]
    s_far = sc[PB:NP, :]
    top = jnp.maximum(jnp.max(s_own, axis=0, keepdims=True), jnp.max(s_far, axis=0, keepdims=True))
    e_own = weights * jnp.exp(s_own - top)
    e_far = jnp.exp(s_far - top)
    total = jnp.sum(e_own, axis=0, keepdims=True) + jnp.sum(e_far, axis=0, keepdims=True)
    stats[ci, 0:1, :] = top
    stats[ci, 1:2, :] = total

    def to_class(ref, i):
        for j in (4, 3, 5, 2, 6, 1, 7, 0):
            remote(ref.at[ci], ref.at[ci], one_s.at[i], one_r.at[i], in_class(j, 1 - c)).start()
            if j:
                remote(ref.at[ci], ref.at[ci], one_s.at[i], one_r.at[i], in_class(j, c)).start()

    def several(ref, i, n):
        part = ref.at[pl.ds(0, n)]
        return remote(part, part, one_s.at[i], one_r.at[i], pp)

    to_class(stats, 3)

    offs = (4, 3, -3, 2, -2, 1, -1, 0)
    slot_after = (None, 3, 4, 5, 6, 7, 0)

    def dest(i, cc):
        return rows(cc * RING + ((r + offs[i]) & 7))

    et[:, 0:PB] = jnp.transpose(e_own).astype(BF16)
    et[:, PB:NP] = jnp.transpose(e_far).astype(BF16)
    theirs = rows(1 - c, RING * QB)
    for f in range(NF):
        dq[f, theirs, :] = jnp.dot(et[theirs, :], pb[f], preferred_element_type=F32).astype(BF16)

    def send_rsy(i0, i1):
        for i in range(i0, i1):
            for f in range(NF):
                remote(dq.at[f, dest(i, 1 - c), :], yr.at[i, f], one_s.at[4], rsy_r.at[i, f], yp).start()

    send_rsy(0, 3)
    pos_score = jnp.sum(is_pos * s_own, axis=0, keepdims=True)
    several(stats, 3, 15).wait_recv()
    top_all = stats[0, 0:1, :]
    for k in range(1, CLASS):
        top_all = jnp.maximum(top_all, stats[k, 0:1, :])
    sum_all = jnp.zeros((1, NQ), F32)
    for k in range(CLASS):
        sum_all = sum_all + stats[k, 1:2, :] * jnp.exp(stats[k, 0:1, :] - top_all)
    log_total = top_all + jnp.log(sum_all)
    lane1 = lax.broadcasted_iota(jnp.int32, (1, NQ), 1)
    loss_part = jnp.sum(
        jnp.where(lane1 // QB == ci, log_total - pos_score, 0.0), axis=1, keepdims=True
    )

    ds[0:PB, :] = (weights * jnp.exp(s_own - log_total) - is_pos).astype(BF16)
    ds[PB:NP, :] = jnp.exp(s_far - log_total).astype(BF16)
    ds_f = ds[...].astype(F32)
    rest = pl.ds(FC, D - FC)

    def dp_first():
        return remote(dps.at[:, pl.ds(0, FC)], dpr.at[:, pl.ds(0, FC)], one_s.at[5], one_r.at[5], pp)

    def dp_block(b):
        return remote(dps.at[rows(b), rest], dpr.at[rows(b), rest], one_s.at[5], dp_r.at[b], pp)

    def start_dp(b, _):
        dp_block(b).start()
        return 0

    for f in range(NF):
        d = LOGIT_SCALE * jnp.dot(ds[...], qb[f], preferred_element_type=F32)
        dp[:, f * FC:(f + 1) * FC] = d[0:PB, :]
        dps[:, f * FC:(f + 1) * FC] = d[PB:NP, :].astype(BF16)
        if f == 0:
            dp_first().start()
    lax.fori_loop(0, 2, start_dp, 0)

    et[...] = jnp.transpose(ds_f).astype(BF16)
    scale = LOGIT_SCALE * jnp.exp(stats[(1 - c) * RING + r, 0:1, :] - log_total)
    from_y[...] = jnp.transpose(jnp.broadcast_to(scale, (8, NQ)))[:, 0:1]
    ours = rows(c, RING * QB)
    for f in range(NF):
        dq[f, ours, :] = (LOGIT_SCALE * jnp.dot(et[ours, :], pb[f], preferred_element_type=F32)).astype(BF16)

    def zr_got(i, f):
        return remote(zs.at[0, f], zr.at[i, f], one_s.at[6], z_r.at[i, f], nxt)

    def ring_step(i):
        for f in range(NF):
            forth = f < NF // 2
            rsy = remote(yr.at[i, f], yr.at[i, f], one_s.at[4], rsy_r.at[i, f], yp)
            rsy.wait_recv()
            acc = dq[f, dest(i, c), :].astype(F32) + yr[i, f].astype(F32) * from_y[dest(i, c), :]
            if i >= 3 or (i == 1 and forth) or (i == 2 and not forth):
                zr_got(i, f).wait_recv()
                acc = acc + zr[i, f].astype(F32)
            zs[i, f] = acc.astype(BF16)
            ahead = forth if i == 0 else i % 2 == 1
            after = (1 if forth else 2) if i == 0 else slot_after[i]
            remote(zs.at[i, f], zr.at[after, f], one_s.at[6], z_r.at[after, f], nxt if ahead else prv).start()

    ring_step(0)

    prod = ds_f * sc[...]
    u = jnp.sum(prod, axis=1, keepdims=True)
    t_row = jnp.sum(prod, axis=0, keepdims=True)
    t = jnp.transpose(jnp.broadcast_to(t_row, (8, NQ)))[:, 0:1]
    for f in range(NF):
        cols = slice(f * FC, (f + 1) * FC)
        p_own = pb[f, 0:PB, :].astype(F32)
        p_far = pb[f, PB:NP, :].astype(F32)
        q_f = qb[f].astype(F32)
        g = (
            jnp.sum(p_own * (2.0 * dp[:, cols] - p_own * u[0:PB]), axis=0, keepdims=True)
            + jnp.sum(p_far * (2.0 * dps[:, cols].astype(F32) - p_far * u[PB:NP]), axis=0, keepdims=True)
            - jnp.sum(q_f * q_f * t, axis=0, keepdims=True)
        ) / gain_ref[:, cols]
        for k in range(FC // SEG):
            ga[f * (FC // SEG) + k, 0:1, :] = g[:, k * SEG:(k + 1) * SEG]
            ga[f * (FC // SEG) + k, 1:2, :] = jnp.broadcast_to(loss_part, (1, SEG))

    def spread(n, to, src_of, dst, i, order=None):
        for k in order or range(1, n):
            dev, other_dy = to(k)
            remote(src_of(k), dst, one_s.at[i], one_r.at[i], dev, other_dy).start()

    def total_of(ref, n):
        out = ref[0]
        for k in range(1, n):
            out = out + ref[k]
        return out

    spread(PLANE, in_plane, lambda k: ga.at[(plane + k) & 31], gar.at[plane], 7)
    gar[plane] = ga[plane]
    lax.fori_loop(2, 4, start_dp, 0)
    send_rsy(3, 5)
    ring_step(1)
    ring_step(2)
    send_rsy(5, 8)
    lax.fori_loop(4, PB // QB, start_dp, 0)

    several(gar, 7, PLANE - 1).wait_recv()
    gc[tall] = total_of(gar, PLANE)
    spread(16, along_z, lambda k: gc.at[tall], gc.at[tall], 9, (8, 7, 9, 6, 10, 5, 11, 4, 12, 3, 13, 2, 14, 1, 15))

    def backward(hidden, inv_rms, inv_len, d):
        g = gain_ref[...]
        unit = hidden.astype(F32) * inv_rms
        e = unit * g * inv_len
        dnormed = inv_len * (d - e * jnp.sum(e * d, axis=1, keepdims=True))
        dunit = dnormed * g
        mean = jnp.sum(dunit * unit, axis=1, keepdims=True) * (1.0 / D)
        return (inv_rms * (dunit - unit * mean)).astype(BF16)

    def p_block(b, _):
        dp_block(b).wait_recv()
        at = rows(b)
        d = dp[at, :] + dpr[at, :].astype(F32)
        pg_v[at, :] = backward(p_ref[at, :], pstat[0, at, :], pstat[1, at, :], d)
        pltpu.make_async_copy(pg_v.at[at, :], pg_ref.at[at, :], in_sem.at[3]).start()
        return 0

    def p_blocks(b0, b1):
        lax.fori_loop(b0, b1, p_block, 0)

    ring_step(3)
    ring_step(4)
    dp_first().wait_recv()
    p_blocks(0, 2)
    several(gc, 9, 15).wait_recv()
    gd[plane] = total_of(gc, 16)
    spread(PLANE, in_plane, lambda k: gd.at[plane], gd.at[plane], 10)
    ring_step(5)
    ring_step(6)
    p_blocks(2, 6)

    for f in range(NF):
        rsy = remote(yr.at[RING - 1, f], yr.at[RING - 1, f], one_s.at[4], rsy_r.at[RING - 1, f], yp)
        rsy.wait_recv()
        zr_got(7, f).wait_recv()
        zr_got(0, f).wait_recv()
        dfin[:, f * FC:(f + 1) * FC] = (
            dq[f, dest(7, c), :].astype(F32) + yr[RING - 1, f].astype(F32) * from_y[dest(7, c), :]
            + (zr[7, f].astype(F32) + zr[0, f].astype(F32))
        )
    _, q_rms, q_len = embed(q_ref[...])
    qg_v[...] = backward(q_ref[...], q_rms, q_len, dfin[...])
    p_blocks(6, 8)

    several(gd, 10, PLANE - 1).wait_recv()
    for k in range(PLANE):
        gg_v[:, k * SEG:(k + 1) * SEG] = gd[k, 0:1, :]
    loss_v[...] = gd[0, 1:2, 0:1]
    stores = [
        pltpu.make_async_copy(src, dst, in_sem.at[i])
        for i, (src, dst) in enumerate(((qg_v, qg_ref), (gg_v, gg_ref), (loss_v, loss_ref)))
    ]
    for store in stores:
        store.start()
    for store in stores:
        store.wait()
    pltpu.make_async_copy(pg_v, pg_ref, in_sem.at[3]).wait()

    for ref, i in (
        (qb.at[:, pl.ds(0, 7 * QB), :], 0), (qb.at[:, pl.ds(0, 8 * QB), :], 1), (far_ref, 2),
        (yr, 4), (dpr, 5), (zs.at[pl.ds(0, 7)], 6),
    ):
        remote(ref, ref, one_s.at[i], one_r.at[i], pp).wait_send()
    for ref, i, n in (
        (stats, 3, 15), (gar, 7, PLANE - 1), (gc, 9, 15), (gd, 10, PLANE - 1)
    ):
        several(ref, i, n).wait_send()


def hand_over(qg_in, pg_in, gg_in, qg_ref, pg_ref, gg_ref, qg_v, pg_v, gg_v, in_sem, out_sem):
    parts = [(qg_in, qg_v, qg_ref), (gg_in, gg_v, gg_ref)]
    for i in range(4):
        at = pl.ds(i * PB // 4, PB // 4)
        parts.append(tuple(ref.at[at, :] for ref in (pg_in, pg_v, pg_ref)))
    loads = [pltpu.make_async_copy(a, b, in_sem.at[i]) for i, (a, b, _) in enumerate(parts)]
    stores = [pltpu.make_async_copy(b, c, out_sem.at[i]) for i, (_, b, c) in enumerate(parts)]
    for load in loads:
        load.start()
    for load, store in zip(loads, stores):
        load.wait()
        store.start()
    for store in stores:
        store.wait()


def on_device(query_hidden, passage_hidden, gain, hard_ids, positive_ids):
    del hard_ids
    hbm = pl.BlockSpec(memory_space=pltpu.HBM)
    any_space = pl.BlockSpec(memory_space=pl.ANY)
    dma = pltpu.SemaphoreType.DMA
    shapes = (
        jax.ShapeDtypeStruct((QB, D), BF16),
        jax.ShapeDtypeStruct((PB, D), BF16),
        jax.ShapeDtypeStruct((1, D), F32),
    )
    query_grad, passage_grad, gain_grad, loss = pl.pallas_call(
        kernel,
        out_shape=(*shapes, jax.ShapeDtypeStruct((1, 1), F32)),
        in_specs=[hbm] * 4,
        out_specs=(any_space,) * 4,
        scratch_shapes=[
            pltpu.VMEM((QB, D), BF16),
            pltpu.VMEM((PB, D), BF16),
            pltpu.VMEM((PB, D), BF16),
            pltpu.VMEM((1, D), F32),
            pltpu.VMEM((1, QB), jnp.int32),
            pltpu.VMEM((NF, NQ, FC), BF16),
            pltpu.VMEM((NF, NP, FC), BF16),
            pltpu.VMEM((NP, NQ), F32),
            pltpu.VMEM((NP, NQ), BF16),
            pltpu.VMEM((NF, NQ, FC), BF16),
            pltpu.VMEM((RING, NF, QB, FC), BF16),
            pltpu.VMEM((RING, NF, QB, FC), BF16),
            pltpu.VMEM((RING, NF, QB, FC), BF16),
            pltpu.VMEM((PB, D), F32),
            pltpu.VMEM((PB, D), BF16),
            pltpu.VMEM((PB, D), BF16),
            pltpu.VMEM((QB, D), F32),
            pltpu.VMEM((2, PB, 1), F32),
            pltpu.VMEM((CLASS, 2, NQ), F32),
            pltpu.VMEM((PLANE, 2, SEG), F32),
            pltpu.VMEM((PLANE, 2, SEG), F32),
            pltpu.VMEM((16, 2, SEG), F32),
            pltpu.VMEM((PLANE, 2, SEG), F32),
            pltpu.VMEM((NQ, NP), BF16),
            pltpu.VMEM((NQ, 1), F32),
            pltpu.VMEM((QB, D), BF16),
            pltpu.VMEM((PB, D), BF16),
            pltpu.VMEM((1, D), F32),
            pltpu.VMEM((1, 1), F32),
            dma((4,)),
            dma((RING, NF)),
            dma((RING, NF)),
            dma((PB // QB,)),
            dma((PB // QB,)),
            dma((NF,)),
            dma((12,)),
            dma((12,)),
        ],
        compiler_params=pltpu.CompilerParams(
            collective_id=0, has_side_effects=True, vmem_limit_bytes=60 * 1024 * 1024
        ),
        cost_estimate=pl.CostEstimate(flops=1_610_612_736, bytes_accessed=2_400_000, transcendentals=200_000),
    )(query_hidden, passage_hidden, gain.reshape(1, D), positive_ids.reshape(1, QB))
    query_grad, passage_grad, gain_grad = pl.pallas_call(
        hand_over,
        out_shape=shapes,
        in_specs=[any_space] * 3,
        out_specs=(any_space,) * 3,
        scratch_shapes=[
            pltpu.VMEM((QB, D), BF16), pltpu.VMEM((PB, D), BF16), pltpu.VMEM((1, D), F32), dma((6,)), dma((6,))
        ],
        compiler_params=pltpu.CompilerParams(vmem_limit_bytes=60 * 1024 * 1024),
    )(query_grad, passage_grad, gain_grad)
    return query_grad, passage_grad, gain_grad.reshape(D), loss.reshape(())


def solution(mesh):
    placed = (
        P(("dx", "dy"), None),
        P(("dx", "dy"), None),
        P(),
        P(("dx", "dy"), None),
        P(("dx", "dy")),
    )
    return jax.shard_map(
        on_device,
        mesh=mesh,
        in_specs=placed,
        out_specs=(P(("dx", "dy"), None), P(("dx", "dy"), None), P(), P()),
        check_vma=False,
    )
```

```python
import jax
import jax.numpy as jnp
from jax import lax
from jax.experimental import pallas as pl
from jax.experimental.pallas import tpu as pltpu
from jax.sharding import PartitionSpec as P

MESH = pl.DeviceIdType.MESH
F32 = jnp.float32
BF16 = jnp.bfloat16

LOGIT_SCALE = 250.0
HARD_WEIGHT = 3.0
D = 4096
QB = 16
PB = 128
RING = 8
CLASS = 16
NQ = QB * CLASS
NP = 2 * PB
NF = 4
FC = D // NF
PLANE = 32
SEG = D // PLANE


def kernel(
    q_hbm, p_hbm, gain_hbm, pos_hbm,
    qg_ref, pg_ref, gg_ref, loss_ref,
    q_ref, p_ref, far_ref, gain_ref, pos_ref,
    qb, pb, sc, ds, dq, yr, zs, zr, dp, dps, dpr, dfin, pstat, stats, ga, gar, gc, gd, et, from_y, qg_v, pg_v, gg_v, loss_v,
    in_sem, z_r, rsy_r, dp_r, px_r, agy_r, one_s, one_r,
):
    dx = lax.axis_index("dx")
    dy = lax.axis_index("dy")
    y = dx & 3
    z = dx >> 2
    half = z >> 1
    r = half + (z & 1) * (7 - 2 * half)
    c = y >> 1
    cls = (y + c) & 1
    ci = c * RING + r

    def z_of(place):
        return 2 * place + (place >> 2) * (15 - 4 * place)

    nxt = z_of((r + 1) & 7) * 4 + y
    prv = z_of((r + 7) & 7) * 4 + y
    yp = z * 4 + 3 - y
    pp = z * 4 + y + 1 - 2 * (y & 1)

    x = dy >> 2
    z_hi = (dy >> 1) & 1
    core = dy & 1
    plane = (x * 2 + core) * 4 + y
    tall = z_hi * RING + z

    def in_plane(k):
        other = (plane + k) & 31
        return z * 4 + (other & 3), (other >> 3) * 4 + z_hi * 2 + ((other >> 2) & 1)

    def along_z(k):
        other = (tall + k) & 15
        return (other & 7) * 4 + y, x * 4 + (other >> 3) * 2 + core

    def in_class(j, cc):
        return z_of((r + j) & 7) * 4 + cls + cc * (3 - 2 * cls)

    def rows(block, size=QB):
        return pl.ds(pl.multiple_of(block * size, size), size)

    def remote(src, dst, send, recv, dev, other_dy=None):
        return pltpu.make_async_remote_copy(
            src_ref=src, dst_ref=dst, send_sem=send, recv_sem=recv,
            device_id=(dev, dy if other_dy is None else other_dy), device_id_type=MESH,
        )

    loads = [
        pltpu.make_async_copy(src, dst, in_sem.at[i])
        for i, (src, dst) in enumerate(
            ((q_hbm, q_ref), (gain_hbm, gain_ref), (pos_hbm, pos_ref), (p_hbm, p_ref))
        )
    ]
    for load in loads:
        load.start()

    barrier = pltpu.get_barrier_semaphore()

    def greet(dev, other_dy):
        pl.semaphore_signal(barrier, inc=1, device_id=(dev, other_dy), device_id_type=MESH)

    for k in range(1, RING):
        greet(in_class(k, 1 - c), dy)
    for k in (8, 7, 9, 6, 10, 5, 11, 4, 12, 3, 13, 2, 14, 1, 15):
        greet(*along_z(k))
    for k in range(1, PLANE):
        greet(*in_plane(k))

    def embed(hidden):
        v = hidden.astype(F32)
        vg = v * gain_ref[...]
        inv_rms = lax.rsqrt(jnp.sum(v * v, axis=1, keepdims=True) * (1.0 / D) + 1e-05)
        inv_len = lax.rsqrt(jnp.sum(vg * vg, axis=1, keepdims=True) * (inv_rms * inv_rms) + 1e-06)
        return vg * (inv_rms * inv_len), inv_rms, inv_len

    loads[0].wait()
    loads[1].wait()
    q_e, _, _ = embed(q_ref[...])
    for f in range(NF):
        qb[f, rows(ci), :] = q_e[:, f * FC:(f + 1) * FC].astype(BF16)

    loads[3].wait()
    pl.semaphore_wait(barrier, 7 + 15 + 31)

    def block(off, f, cc=None):
        return qb.at[f, rows((c if cc is None else cc) * RING + ((r + off) & 7)), :]

    def send_f(h, f):
        return remote(block(-h, f), block(-h, f), one_s.at[0], z_r.at[2 * h, f], nxt)

    def send_b(h, f):
        return remote(block(h, f), block(h, f), one_s.at[0], z_r.at[2 * h + 1, f], prv)

    def got_f(h, f):
        return remote(block(-h, f), block(-h, f), one_s.at[0], z_r.at[2 * h - 2, f], nxt)

    def got_b(h, f):
        return remote(block(h, f), block(h, f), one_s.at[0], z_r.at[2 * h - 1, f], prv)

    def send_y(off, f):
        return remote(block(off, f), block(off, f), one_s.at[1], agy_r.at[f], yp)

    def swap(b):
        return remote(p_ref.at[rows(b), :], far_ref.at[rows(b), :], one_s.at[2], px_r.at[b], pp)

    swap(0).start()
    swap(1).start()
    for f in range(NF):
        send_f(0, f).start()
        send_b(0, f).start()
        send_y(0, f).start()
    for b in range(2, PB // QB):
        swap(b).start()

    def embed_block(b, _):
        e, inv_rms, inv_len = embed(p_ref[rows(b), :])
        for f in range(NF):
            pb[f, rows(b), :] = e[:, f * FC:(f + 1) * FC].astype(BF16)
        pstat[0, rows(b), :] = inv_rms
        pstat[1, rows(b), :] = inv_len
        return 0

    def embed_far(b, _):
        swap(b).wait_recv()
        e, _, _ = embed(far_ref[rows(b), :])
        for f in range(NF):
            pb[f, rows(b + PB // QB), :] = e[:, f * FC:(f + 1) * FC].astype(BF16)
        return 0

    lax.fori_loop(0, PB // QB, embed_block, 0)

    loads[2].wait()
    lane = lax.broadcasted_iota(jnp.int32, (PB, NQ), 1)
    row = lax.broadcasted_iota(jnp.int32, (PB, NQ), 0)
    own = (lane == ci * QB + row // 8).astype(F32)
    ids = lax.broadcasted_iota(jnp.int32, (PB, QB), 0) + dx * PB
    flag = jnp.sum((ids == pos_ref[...]).astype(F32), axis=1, keepdims=True)

    for h in range(1, 5):
        for f in range(NF):
            forth = f < NF // 2
            if h < 4 or forth:
                got_f(h, f).wait_recv()
                if h < 3 or (h == 3 and forth):
                    send_f(h, f).start()
                send_y(-h, f).start()
            if h < 4 or not forth:
                got_b(h, f).wait_recv()
                if h < 3 or (h == 3 and not forth):
                    send_b(h, f).start()
                send_y(h, f).start()
        lax.fori_loop(max(2 * h - 3, 0), 8 if h == 4 else 2 * h - 1, embed_far, 0)

    for f in range(NF):
        arrived = qb.at[f, rows(1 - c, RING * QB), :]
        remote(arrived, arrived, one_s.at[1], agy_r.at[f], yp).wait_recv()
        part = lax.dot_general(pb[f], qb[f], (((1,), (1,)), ((), ())), preferred_element_type=F32)
        sc[...] = part if f == 0 else sc[...] + part
    sc[...] = sc[...] * LOGIT_SCALE

    is_pos = own * flag
    weights = 1.0 + HARD_WEIGHT * (own - is_pos)
    s_own = sc[0:PB, :]
    s_far = sc[PB:NP, :]
    top = jnp.maximum(jnp.max(s_own, axis=0, keepdims=True), jnp.max(s_far, axis=0, keepdims=True))
    e_own = weights * jnp.exp(s_own - top)
    e_far = jnp.exp(s_far - top)
    total = jnp.sum(e_own, axis=0, keepdims=True) + jnp.sum(e_far, axis=0, keepdims=True)
    stats[ci, 0:1, :] = top
    stats[ci, 1:2, :] = total

    def to_class(ref, i):
        for j in (4, 3, 5, 2, 6, 1, 7, 0):
            remote(ref.at[ci], ref.at[ci], one_s.at[i], one_r.at[i], in_class(j, 1 - c)).start()
            if j:
                remote(ref.at[ci], ref.at[ci], one_s.at[i], one_r.at[i], in_class(j, c)).start()

    def several(ref, i, n):
        part = ref.at[pl.ds(0, n)]
        return remote(part, part, one_s.at[i], one_r.at[i], pp)

    to_class(stats, 3)

    offs = (4, 3, -3, 2, -2, 1, -1, 0)
    slot_after = (None, 3, 4, 5, 6, 7, 0)

    def dest(i, cc):
        return rows(cc * RING + ((r + offs[i]) & 7))

    et[:, 0:PB] = jnp.transpose(e_own).astype(BF16)
    et[:, PB:NP] = jnp.transpose(e_far).astype(BF16)
    theirs = rows(1 - c, RING * QB)
    for f in range(NF):
        dq[f, theirs, :] = jnp.dot(et[theirs, :], pb[f], preferred_element_type=F32).astype(BF16)

    def send_rsy(i0, i1):
        for i in range(i0, i1):
            for f in range(NF):
                remote(dq.at[f, dest(i, 1 - c), :], yr.at[i, f], one_s.at[4], rsy_r.at[i, f], yp).start()

    send_rsy(0, 2)
    pos_score = jnp.sum(is_pos * s_own, axis=0, keepdims=True)
    several(stats, 3, 15).wait_recv()
    top_all = stats[0, 0:1, :]
    for k in range(1, CLASS):
        top_all = jnp.maximum(top_all, stats[k, 0:1, :])
    sum_all = jnp.zeros((1, NQ), F32)
    for k in range(CLASS):
        sum_all = sum_all + stats[k, 1:2, :] * jnp.exp(stats[k, 0:1, :] - top_all)
    log_total = top_all + jnp.log(sum_all)
    lane1 = lax.broadcasted_iota(jnp.int32, (1, NQ), 1)
    loss_part = jnp.sum(
        jnp.where(lane1 // QB == ci, log_total - pos_score, 0.0), axis=1, keepdims=True
    )

    ds[0:PB, :] = (weights * jnp.exp(s_own - log_total) - is_pos).astype(BF16)
    ds[PB:NP, :] = jnp.exp(s_far - log_total).astype(BF16)
    ds_f = ds[...].astype(F32)
    rest = pl.ds(FC, D - FC)

    def dp_first():
        return remote(dps.at[:, pl.ds(0, FC)], dpr.at[:, pl.ds(0, FC)], one_s.at[5], one_r.at[5], pp)

    def dp_block(b):
        return remote(dps.at[rows(b), rest], dpr.at[rows(b), rest], one_s.at[5], dp_r.at[b], pp)

    def start_dp(b, _):
        dp_block(b).start()
        return 0

    for f in range(NF):
        d = LOGIT_SCALE * jnp.dot(ds[...], qb[f], preferred_element_type=F32)
        dp[:, f * FC:(f + 1) * FC] = d[0:PB, :]
        dps[:, f * FC:(f + 1) * FC] = d[PB:NP, :].astype(BF16)
        if f == 0:
            dp_first().start()

    et[...] = jnp.transpose(ds_f).astype(BF16)
    scale = LOGIT_SCALE * jnp.exp(stats[(1 - c) * RING + r, 0:1, :] - log_total)
    from_y[...] = jnp.transpose(jnp.broadcast_to(scale, (8, NQ)))[:, 0:1]
    ours = rows(c, RING * QB)
    for f in range(NF):
        dq[f, ours, :] = (LOGIT_SCALE * jnp.dot(et[ours, :], pb[f], preferred_element_type=F32)).astype(BF16)

    def zr_got(i, f):
        return remote(zs.at[0, f], zr.at[i, f], one_s.at[6], z_r.at[i, f], nxt)

    def ring_step(i):
        for f in range(NF):
            forth = f < NF // 2
            rsy = remote(yr.at[i, f], yr.at[i, f], one_s.at[4], rsy_r.at[i, f], yp)
            rsy.wait_recv()
            acc = dq[f, dest(i, c), :].astype(F32) + yr[i, f].astype(F32) * from_y[dest(i, c), :]
            if i >= 3 or (i == 1 and forth) or (i == 2 and not forth):
                zr_got(i, f).wait_recv()
                acc = acc + zr[i, f].astype(F32)
            zs[i, f] = acc.astype(BF16)
            ahead = forth if i == 0 else i % 2 == 1
            after = (1 if forth else 2) if i == 0 else slot_after[i]
            remote(zs.at[i, f], zr.at[after, f], one_s.at[6], z_r.at[after, f], nxt if ahead else prv).start()

    ring_step(0)

    prod = ds_f * sc[...]
    u = jnp.sum(prod, axis=1, keepdims=True)
    t_row = jnp.sum(prod, axis=0, keepdims=True)
    t = jnp.transpose(jnp.broadcast_to(t_row, (8, NQ)))[:, 0:1]
    for f in range(NF):
        cols = slice(f * FC, (f + 1) * FC)
        p_own = pb[f, 0:PB, :].astype(F32)
        p_far = pb[f, PB:NP, :].astype(F32)
        q_f = qb[f].astype(F32)
        g = (
            jnp.sum(p_own * (2.0 * dp[:, cols] - p_own * u[0:PB]), axis=0, keepdims=True)
            + jnp.sum(p_far * (2.0 * dps[:, cols].astype(F32) - p_far * u[PB:NP]), axis=0, keepdims=True)
            - jnp.sum(q_f * q_f * t, axis=0, keepdims=True)
        ) / gain_ref[:, cols]
        for k in range(FC // SEG):
            ga[f * (FC // SEG) + k, 0:1, :] = g[:, k * SEG:(k + 1) * SEG]
            ga[f * (FC // SEG) + k, 1:2, :] = jnp.broadcast_to(loss_part, (1, SEG))

    def spread(n, to, src_of, dst, i, order=None):
        for k in order or range(1, n):
            dev, other_dy = to(k)
            remote(src_of(k), dst, one_s.at[i], one_r.at[i], dev, other_dy).start()

    def total_of(ref, n):
        out = ref[0]
        for k in range(1, n):
            out = out + ref[k]
        return out

    spread(PLANE, in_plane, lambda k: ga.at[(plane + k) & 31], gar.at[plane], 7)
    gar[plane] = ga[plane]
    dp_block(0).start()
    send_rsy(2, 4)
    ring_step(1)
    dp_block(1).start()
    send_rsy(4, 5)
    ring_step(2)
    lax.fori_loop(2, 4, start_dp, 0)

    several(gar, 7, PLANE - 1).wait_recv()
    gc[tall] = total_of(gar, PLANE)
    spread(16, along_z, lambda k: gc.at[tall], gc.at[tall], 9, (8, 7, 9, 6, 10, 5, 11, 4, 12, 3, 13, 2, 14, 1, 15))

    def backward(hidden, inv_rms, inv_len, d):
        g = gain_ref[...]
        unit = hidden.astype(F32) * inv_rms
        e = unit * g * inv_len
        dnormed = inv_len * (d - e * jnp.sum(e * d, axis=1, keepdims=True))
        dunit = dnormed * g
        mean = jnp.sum(dunit * unit, axis=1, keepdims=True) * (1.0 / D)
        return (inv_rms * (dunit - unit * mean)).astype(BF16)

    def p_block(b, _):
        dp_block(b).wait_recv()
        at = rows(b)
        d = dp[at, :] + dpr[at, :].astype(F32)
        pg_v[at, :] = backward(p_ref[at, :], pstat[0, at, :], pstat[1, at, :], d)
        pltpu.make_async_copy(pg_v.at[at, :], pg_ref.at[at, :], in_sem.at[3]).start()
        return 0

    def p_blocks(b0, b1):
        lax.fori_loop(b0, b1, p_block, 0)

    ring_step(3)
    send_rsy(5, 7)
    dp_block(4).start()
    ring_step(4)
    dp_block(5).start()
    dp_first().wait_recv()
    p_blocks(0, 2)
    ring_step(5)
    several(gc, 9, 15).wait_recv()
    gd[plane] = total_of(gc, 16)
    spread(PLANE, in_plane, lambda k: gd.at[plane], gd.at[plane], 10)
    lax.fori_loop(6, 8, start_dp, 0)
    send_rsy(7, 8)
    ring_step(6)
    p_blocks(2, 6)

    for f in range(NF):
        rsy = remote(yr.at[RING - 1, f], yr.at[RING - 1, f], one_s.at[4], rsy_r.at[RING - 1, f], yp)
        rsy.wait_recv()
        zr_got(7, f).wait_recv()
        zr_got(0, f).wait_recv()
        dfin[:, f * FC:(f + 1) * FC] = (
            dq[f, dest(7, c), :].astype(F32) + yr[RING - 1, f].astype(F32) * from_y[dest(7, c), :]
            + (zr[7, f].astype(F32) + zr[0, f].astype(F32))
        )
    _, q_rms, q_len = embed(q_ref[...])
    qg_v[...] = backward(q_ref[...], q_rms, q_len, dfin[...])
    p_blocks(6, 8)

    several(gd, 10, PLANE - 1).wait_recv()
    for k in range(PLANE):
        gg_v[:, k * SEG:(k + 1) * SEG] = gd[k, 0:1, :]
    loss_v[...] = gd[0, 1:2, 0:1]
    stores = [
        pltpu.make_async_copy(src, dst, in_sem.at[i])
        for i, (src, dst) in enumerate(((qg_v, qg_ref), (gg_v, gg_ref), (loss_v, loss_ref)))
    ]
    for store in stores:
        store.start()
    for store in stores:
        store.wait()
    pltpu.make_async_copy(pg_v, pg_ref, in_sem.at[3]).wait()

    for ref, i in (
        (qb.at[:, pl.ds(0, 7 * QB), :], 0), (qb.at[:, pl.ds(0, 8 * QB), :], 1), (far_ref, 2),
        (yr, 4), (dpr, 5), (zs.at[pl.ds(0, 7)], 6),
    ):
        remote(ref, ref, one_s.at[i], one_r.at[i], pp).wait_send()
    for ref, i, n in (
        (stats, 3, 15), (gar, 7, PLANE - 1), (gc, 9, 15), (gd, 10, PLANE - 1)
    ):
        several(ref, i, n).wait_send()


def hand_over(qg_in, pg_in, gg_in, qg_ref, pg_ref, gg_ref, qg_v, pg_v, gg_v, in_sem, out_sem):
    parts = [(qg_in, qg_v, qg_ref), (gg_in, gg_v, gg_ref)]
    for i in range(4):
        at = pl.ds(i * PB // 4, PB // 4)
        parts.append(tuple(ref.at[at, :] for ref in (pg_in, pg_v, pg_ref)))
    loads = [pltpu.make_async_copy(a, b, in_sem.at[i]) for i, (a, b, _) in enumerate(parts)]
    stores = [pltpu.make_async_copy(b, c, out_sem.at[i]) for i, (_, b, c) in enumerate(parts)]
    for load in loads:
        load.start()
    for load, store in zip(loads, stores):
        load.wait()
        store.start()
    for store in stores:
        store.wait()


def on_device(query_hidden, passage_hidden, gain, hard_ids, positive_ids):
    del hard_ids
    hbm = pl.BlockSpec(memory_space=pltpu.HBM)
    any_space = pl.BlockSpec(memory_space=pl.ANY)
    dma = pltpu.SemaphoreType.DMA
    shapes = (
        jax.ShapeDtypeStruct((QB, D), BF16),
        jax.ShapeDtypeStruct((PB, D), BF16),
        jax.ShapeDtypeStruct((1, D), F32),
    )
    query_grad, passage_grad, gain_grad, loss = pl.pallas_call(
        kernel,
        out_shape=(*shapes, jax.ShapeDtypeStruct((1, 1), F32)),
        in_specs=[hbm] * 4,
        out_specs=(any_space,) * 4,
        scratch_shapes=[
            pltpu.VMEM((QB, D), BF16),
            pltpu.VMEM((PB, D), BF16),
            pltpu.VMEM((PB, D), BF16),
            pltpu.VMEM((1, D), F32),
            pltpu.VMEM((1, QB), jnp.int32),
            pltpu.VMEM((NF, NQ, FC), BF16),
            pltpu.VMEM((NF, NP, FC), BF16),
            pltpu.VMEM((NP, NQ), F32),
            pltpu.VMEM((NP, NQ), BF16),
            pltpu.VMEM((NF, NQ, FC), BF16),
            pltpu.VMEM((RING, NF, QB, FC), BF16),
            pltpu.VMEM((RING, NF, QB, FC), BF16),
            pltpu.VMEM((RING, NF, QB, FC), BF16),
            pltpu.VMEM((PB, D), F32),
            pltpu.VMEM((PB, D), BF16),
            pltpu.VMEM((PB, D), BF16),
            pltpu.VMEM((QB, D), F32),
            pltpu.VMEM((2, PB, 1), F32),
            pltpu.VMEM((CLASS, 2, NQ), F32),
            pltpu.VMEM((PLANE, 2, SEG), F32),
            pltpu.VMEM((PLANE, 2, SEG), F32),
            pltpu.VMEM((16, 2, SEG), F32),
            pltpu.VMEM((PLANE, 2, SEG), F32),
            pltpu.VMEM((NQ, NP), BF16),
            pltpu.VMEM((NQ, 1), F32),
            pltpu.VMEM((QB, D), BF16),
            pltpu.VMEM((PB, D), BF16),
            pltpu.VMEM((1, D), F32),
            pltpu.VMEM((1, 1), F32),
            dma((4,)),
            dma((RING, NF)),
            dma((RING, NF)),
            dma((PB // QB,)),
            dma((PB // QB,)),
            dma((NF,)),
            dma((12,)),
            dma((12,)),
        ],
        compiler_params=pltpu.CompilerParams(
            collective_id=0, has_side_effects=True, vmem_limit_bytes=60 * 1024 * 1024
        ),
        cost_estimate=pl.CostEstimate(flops=1_610_612_736, bytes_accessed=2_400_000, transcendentals=200_000),
    )(query_hidden, passage_hidden, gain.reshape(1, D), positive_ids.reshape(1, QB))
    query_grad, passage_grad, gain_grad = pl.pallas_call(
        hand_over,
        out_shape=shapes,
        in_specs=[any_space] * 3,
        out_specs=(any_space,) * 3,
        scratch_shapes=[
            pltpu.VMEM((QB, D), BF16), pltpu.VMEM((PB, D), BF16), pltpu.VMEM((1, D), F32), dma((6,)), dma((6,))
        ],
        compiler_params=pltpu.CompilerParams(vmem_limit_bytes=60 * 1024 * 1024),
    )(query_grad, passage_grad, gain_grad)
    return query_grad, passage_grad, gain_grad.reshape(D), loss.reshape(())


def solution(mesh):
    placed = (
        P(("dx", "dy"), None),
        P(("dx", "dy"), None),
        P(),
        P(("dx", "dy"), None),
        P(("dx", "dy")),
    )
    return jax.shard_map(
        on_device,
        mesh=mesh,
        in_specs=placed,
        out_specs=(P(("dx", "dy"), None), P(("dx", "dy"), None), P(), P()),
        check_vma=False,
    )
```

```python
import jax
import jax.numpy as jnp
from jax import lax
from jax.experimental import pallas as pl
from jax.experimental.pallas import tpu as pltpu
from jax.sharding import PartitionSpec as P

MESH = pl.DeviceIdType.MESH
F32 = jnp.float32
BF16 = jnp.bfloat16

LOGIT_SCALE = 250.0
HARD_WEIGHT = 3.0
D = 4096
QB = 16
PB = 128
RING = 8
CLASS = 16
NQ = QB * CLASS
NP = 2 * PB
NF = 4
FC = D // NF
PLANE = 32
SEG = D // PLANE


def kernel(
    q_hbm, p_hbm, gain_hbm, pos_hbm,
    qg_ref, pg_ref, gg_ref, loss_ref,
    q_ref, p_ref, far_ref, gain_ref, pos_ref,
    qb, pb, sc, ds, dq, yr, zs, zr, dp, dps, dpr, dfin, pstat, stats, ga, gar, gc, gd, et, from_y, qg_v, pg_v, gg_v, loss_v,
    in_sem, z_r, rsy_r, dp_r, px_r, agy_r, one_s, one_r,
):
    dx = lax.axis_index("dx")
    dy = lax.axis_index("dy")
    y = dx & 3
    z = dx >> 2
    half = z >> 1
    r = half + (z & 1) * (7 - 2 * half)
    c = y >> 1
    cls = (y + c) & 1
    ci = c * RING + r

    def z_of(place):
        return 2 * place + (place >> 2) * (15 - 4 * place)

    nxt = z_of((r + 1) & 7) * 4 + y
    prv = z_of((r + 7) & 7) * 4 + y
    yp = z * 4 + 3 - y
    pp = z * 4 + y + 1 - 2 * (y & 1)

    x = dy >> 2
    z_hi = (dy >> 1) & 1
    core = dy & 1
    plane = (x * 2 + core) * 4 + y
    tall = z_hi * RING + z

    def in_plane(k):
        other = (plane + k) & 31
        return z * 4 + (other & 3), (other >> 3) * 4 + z_hi * 2 + ((other >> 2) & 1)

    def along_z(k):
        other = (tall + k) & 15
        return (other & 7) * 4 + y, x * 4 + (other >> 3) * 2 + core

    def in_class(j, cc):
        return z_of((r + j) & 7) * 4 + cls + cc * (3 - 2 * cls)

    def rows(block, size=QB):
        return pl.ds(pl.multiple_of(block * size, size), size)

    def remote(src, dst, send, recv, dev, other_dy=None):
        return pltpu.make_async_remote_copy(
            src_ref=src, dst_ref=dst, send_sem=send, recv_sem=recv,
            device_id=(dev, dy if other_dy is None else other_dy), device_id_type=MESH,
        )

    loads = [
        pltpu.make_async_copy(src, dst, in_sem.at[i])
        for i, (src, dst) in enumerate(
            ((q_hbm, q_ref), (gain_hbm, gain_ref), (pos_hbm, pos_ref), (p_hbm, p_ref))
        )
    ]
    for load in loads:
        load.start()

    barrier = pltpu.get_barrier_semaphore()

    def greet(dev, other_dy):
        pl.semaphore_signal(barrier, inc=1, device_id=(dev, other_dy), device_id_type=MESH)

    for k in range(1, RING):
        greet(in_class(k, 1 - c), dy)
    for k in (8, 7, 9, 6, 10, 5, 11, 4, 12, 3, 13, 2, 14, 1, 15):
        greet(*along_z(k))
    for k in range(1, PLANE):
        greet(*in_plane(k))

    def embed(hidden):
        v = hidden.astype(F32)
        vg = v * gain_ref[...]
        inv_rms = lax.rsqrt(jnp.sum(v * v, axis=1, keepdims=True) * (1.0 / D) + 1e-05)
        inv_len = lax.rsqrt(jnp.sum(vg * vg, axis=1, keepdims=True) * (inv_rms * inv_rms) + 1e-06)
        return vg * (inv_rms * inv_len), inv_rms, inv_len

    loads[0].wait()
    loads[1].wait()
    q_e, _, _ = embed(q_ref[...])
    for f in range(NF):
        qb[f, rows(ci), :] = q_e[:, f * FC:(f + 1) * FC].astype(BF16)

    loads[3].wait()
    pl.semaphore_wait(barrier, 7 + 15 + 31)

    def block(off, f, cc=None):
        return qb.at[f, rows((c if cc is None else cc) * RING + ((r + off) & 7)), :]

    def send_f(h, f):
        return remote(block(-h, f), block(-h, f), one_s.at[0], z_r.at[2 * h, f], nxt)

    def send_b(h, f):
        return remote(block(h, f), block(h, f), one_s.at[0], z_r.at[2 * h + 1, f], prv)

    def got_f(h, f):
        return remote(block(-h, f), block(-h, f), one_s.at[0], z_r.at[2 * h - 2, f], nxt)

    def got_b(h, f):
        return remote(block(h, f), block(h, f), one_s.at[0], z_r.at[2 * h - 1, f], prv)

    def send_y(off, f):
        return remote(block(off, f), block(off, f), one_s.at[1], agy_r.at[f], yp)

    def swap(b):
        return remote(p_ref.at[rows(b), :], far_ref.at[rows(b), :], one_s.at[2], px_r.at[b], pp)

    swap(0).start()
    swap(1).start()
    for f in range(NF):
        send_f(0, f).start()
        send_b(0, f).start()
        send_y(0, f).start()
    for b in range(2, PB // QB):
        swap(b).start()

    def embed_block(b, _):
        e, inv_rms, inv_len = embed(p_ref[rows(b), :])
        for f in range(NF):
            pb[f, rows(b), :] = e[:, f * FC:(f + 1) * FC].astype(BF16)
        pstat[0, rows(b), :] = inv_rms
        pstat[1, rows(b), :] = inv_len
        return 0

    def embed_far(b, _):
        swap(b).wait_recv()
        e, _, _ = embed(far_ref[rows(b), :])
        for f in range(NF):
            pb[f, rows(b + PB // QB), :] = e[:, f * FC:(f + 1) * FC].astype(BF16)
        return 0

    lax.fori_loop(0, PB // QB, embed_block, 0)

    loads[2].wait()
    lane = lax.broadcasted_iota(jnp.int32, (PB, NQ), 1)
    row = lax.broadcasted_iota(jnp.int32, (PB, NQ), 0)
    own = (lane == ci * QB + row // 8).astype(F32)
    ids = lax.broadcasted_iota(jnp.int32, (PB, QB), 0) + dx * PB
    flag = jnp.sum((ids == pos_ref[...]).astype(F32), axis=1, keepdims=True)

    for h in range(1, 5):
        for f in range(NF):
            forth = f < NF // 2
            if h < 4 or forth:
                got_f(h, f).wait_recv()
                if h < 3 or (h == 3 and forth):
                    send_f(h, f).start()
                send_y(-h, f).start()
            if h < 4 or not forth:
                got_b(h, f).wait_recv()
                if h < 3 or (h == 3 and not forth):
                    send_b(h, f).start()
                send_y(h, f).start()
        lax.fori_loop(max(2 * h - 4, 0), 8 if h == 4 else 2 * h - 2, embed_far, 0)

    for f in range(NF):
        arrived = qb.at[f, rows(1 - c, RING * QB), :]
        remote(arrived, arrived, one_s.at[1], agy_r.at[f], yp).wait_recv()
        part = lax.dot_general(pb[f], qb[f], (((1,), (1,)), ((), ())), preferred_element_type=F32)
        sc[...] = part if f == 0 else sc[...] + part
    sc[...] = sc[...] * LOGIT_SCALE

    is_pos = own * flag
    weights = 1.0 + HARD_WEIGHT * (own - is_pos)
    s_own = sc[0:PB, :]
    s_far = sc[PB:NP, :]
    top = jnp.maximum(jnp.max(s_own, axis=0, keepdims=True), jnp.max(s_far, axis=0, keepdims=True))
    e_own = weights * jnp.exp(s_own - top)
    e_far = jnp.exp(s_far - top)
    total = jnp.sum(e_own, axis=0, keepdims=True) + jnp.sum(e_far, axis=0, keepdims=True)
    stats[ci, 0:1, :] = top
    stats[ci, 1:2, :] = total

    def to_class(ref, i):
        for j in (4, 3, 5, 2, 6, 1, 7, 0):
            remote(ref.at[ci], ref.at[ci], one_s.at[i], one_r.at[i], in_class(j, 1 - c)).start()
            if j:
                remote(ref.at[ci], ref.at[ci], one_s.at[i], one_r.at[i], in_class(j, c)).start()

    def several(ref, i, n):
        part = ref.at[pl.ds(0, n)]
        return remote(part, part, one_s.at[i], one_r.at[i], pp)

    to_class(stats, 3)

    offs = (4, 3, -3, 2, -2, 1, -1, 0)
    slot_after = (None, 3, 4, 5, 6, 7, 0)

    def dest(i, cc):
        return rows(cc * RING + ((r + offs[i]) & 7))

    et[:, 0:PB] = jnp.transpose(e_own).astype(BF16)
    et[:, PB:NP] = jnp.transpose(e_far).astype(BF16)
    theirs = rows(1 - c, RING * QB)
    for f in range(NF):
        dq[f, theirs, :] = jnp.dot(et[theirs, :], pb[f], preferred_element_type=F32).astype(BF16)

    def send_rsy(i0, i1):
        for i in range(i0, i1):
            for f in range(NF):
                remote(dq.at[f, dest(i, 1 - c), :], yr.at[i, f], one_s.at[4], rsy_r.at[i, f], yp).start()

    send_rsy(0, 2)
    pos_score = jnp.sum(is_pos * s_own, axis=0, keepdims=True)
    several(stats, 3, 15).wait_recv()
    top_all = stats[0, 0:1, :]
    for k in range(1, CLASS):
        top_all = jnp.maximum(top_all, stats[k, 0:1, :])
    sum_all = jnp.zeros((1, NQ), F32)
    for k in range(CLASS):
        sum_all = sum_all + stats[k, 1:2, :] * jnp.exp(stats[k, 0:1, :] - top_all)
    log_total = top_all + jnp.log(sum_all)
    lane1 = lax.broadcasted_iota(jnp.int32, (1, NQ), 1)
    loss_part = jnp.sum(
        jnp.where(lane1 // QB == ci, log_total - pos_score, 0.0), axis=1, keepdims=True
    )

    ds[0:PB, :] = (weights * jnp.exp(s_own - log_total) - is_pos).astype(BF16)
    ds[PB:NP, :] = jnp.exp(s_far - log_total).astype(BF16)
    ds_f = ds[...].astype(F32)
    rest = pl.ds(FC, D - FC)

    def dp_first():
        return remote(dps.at[:, pl.ds(0, FC)], dpr.at[:, pl.ds(0, FC)], one_s.at[5], one_r.at[5], pp)

    def dp_block(b):
        return remote(dps.at[rows(b), rest], dpr.at[rows(b), rest], one_s.at[5], dp_r.at[b], pp)

    def start_dp(b, _):
        dp_block(b).start()
        return 0

    for f in range(NF):
        d = LOGIT_SCALE * jnp.dot(ds[...], qb[f], preferred_element_type=F32)
        dp[:, f * FC:(f + 1) * FC] = d[0:PB, :]
        dps[:, f * FC:(f + 1) * FC] = d[PB:NP, :].astype(BF16)
        if f == 0:
            dp_first().start()

    et[...] = jnp.transpose(ds_f).astype(BF16)
    scale = LOGIT_SCALE * jnp.exp(stats[(1 - c) * RING + r, 0:1, :] - log_total)
    from_y[...] = jnp.transpose(jnp.broadcast_to(scale, (8, NQ)))[:, 0:1]
    ours = rows(c, RING * QB)
    for f in range(NF):
        dq[f, ours, :] = (LOGIT_SCALE * jnp.dot(et[ours, :], pb[f], preferred_element_type=F32)).astype(BF16)

    def zr_got(i, f):
        return remote(zs.at[0, f], zr.at[i, f], one_s.at[6], z_r.at[i, f], nxt)

    def ring_step(i):
        for f in range(NF):
            forth = f < NF // 2
            rsy = remote(yr.at[i, f], yr.at[i, f], one_s.at[4], rsy_r.at[i, f], yp)
            rsy.wait_recv()
            acc = dq[f, dest(i, c), :].astype(F32) + yr[i, f].astype(F32) * from_y[dest(i, c), :]
            if i >= 3 or (i == 1 and forth) or (i == 2 and not forth):
                zr_got(i, f).wait_recv()
                acc = acc + zr[i, f].astype(F32)
            zs[i, f] = acc.astype(BF16)
            ahead = forth if i == 0 else i % 2 == 1
            after = (1 if forth else 2) if i == 0 else slot_after[i]
            remote(zs.at[i, f], zr.at[after, f], one_s.at[6], z_r.at[after, f], nxt if ahead else prv).start()

    ring_step(0)

    prod = ds_f * sc[...]
    u = jnp.sum(prod, axis=1, keepdims=True)
    t_row = jnp.sum(prod, axis=0, keepdims=True)
    t = jnp.transpose(jnp.broadcast_to(t_row, (8, NQ)))[:, 0:1]
    for f in range(NF):
        cols = slice(f * FC, (f + 1) * FC)
        p_own = pb[f, 0:PB, :].astype(F32)
        p_far = pb[f, PB:NP, :].astype(F32)
        q_f = qb[f].astype(F32)
        g = (
            jnp.sum(p_own * (2.0 * dp[:, cols] - p_own * u[0:PB]), axis=0, keepdims=True)
            + jnp.sum(p_far * (2.0 * dps[:, cols].astype(F32) - p_far * u[PB:NP]), axis=0, keepdims=True)
            - jnp.sum(q_f * q_f * t, axis=0, keepdims=True)
        ) / gain_ref[:, cols]
        for k in range(FC // SEG):
            ga[f * (FC // SEG) + k, 0:1, :] = g[:, k * SEG:(k + 1) * SEG]
            ga[f * (FC // SEG) + k, 1:2, :] = jnp.broadcast_to(loss_part, (1, SEG))

    def spread(n, to, src_of, dst, i, order=None):
        for k in order or range(1, n):
            dev, other_dy = to(k)
            remote(src_of(k), dst, one_s.at[i], one_r.at[i], dev, other_dy).start()

    def total_of(ref, n):
        out = ref[0]
        for k in range(1, n):
            out = out + ref[k]
        return out

    spread(PLANE, in_plane, lambda k: ga.at[(plane + k) & 31], gar.at[plane], 7)
    gar[plane] = ga[plane]
    dp_block(0).start()
    send_rsy(2, 4)
    ring_step(1)
    dp_block(1).start()
    send_rsy(4, 5)
    ring_step(2)
    lax.fori_loop(2, 4, start_dp, 0)

    several(gar, 7, PLANE - 1).wait_recv()
    gc[tall] = total_of(gar, PLANE)
    spread(16, along_z, lambda k: gc.at[tall], gc.at[tall], 9, (8, 7, 9, 6, 10, 5, 11, 4, 12, 3, 13, 2, 14, 1, 15))

    def backward(hidden, inv_rms, inv_len, d):
        g = gain_ref[...]
        unit = hidden.astype(F32) * inv_rms
        e = unit * g * inv_len
        dnormed = inv_len * (d - e * jnp.sum(e * d, axis=1, keepdims=True))
        dunit = dnormed * g
        mean = jnp.sum(dunit * unit, axis=1, keepdims=True) * (1.0 / D)
        return (inv_rms * (dunit - unit * mean)).astype(BF16)

    def p_block(b, _):
        dp_block(b).wait_recv()
        at = rows(b)
        d = dp[at, :] + dpr[at, :].astype(F32)
        pg_v[at, :] = backward(p_ref[at, :], pstat[0, at, :], pstat[1, at, :], d)
        pltpu.make_async_copy(pg_v.at[at, :], pg_ref.at[at, :], in_sem.at[3]).start()
        return 0

    def p_blocks(b0, b1):
        lax.fori_loop(b0, b1, p_block, 0)

    ring_step(3)
    send_rsy(5, 7)
    dp_block(4).start()
    ring_step(4)
    dp_block(5).start()
    dp_first().wait_recv()
    p_blocks(0, 2)
    ring_step(5)
    several(gc, 9, 15).wait_recv()
    gd[plane] = total_of(gc, 16)
    spread(PLANE, in_plane, lambda k: gd.at[plane], gd.at[plane], 10)
    lax.fori_loop(6, 8, start_dp, 0)
    send_rsy(7, 8)
    ring_step(6)
    p_blocks(2, 6)

    for f in range(NF):
        rsy = remote(yr.at[RING - 1, f], yr.at[RING - 1, f], one_s.at[4], rsy_r.at[RING - 1, f], yp)
        rsy.wait_recv()
        zr_got(7, f).wait_recv()
        zr_got(0, f).wait_recv()
        dfin[:, f * FC:(f + 1) * FC] = (
            dq[f, dest(7, c), :].astype(F32) + yr[RING - 1, f].astype(F32) * from_y[dest(7, c), :]
            + (zr[7, f].astype(F32) + zr[0, f].astype(F32))
        )
    _, q_rms, q_len = embed(q_ref[...])
    qg_v[...] = backward(q_ref[...], q_rms, q_len, dfin[...])
    p_blocks(6, 8)

    several(gd, 10, PLANE - 1).wait_recv()
    for k in range(PLANE):
        gg_v[:, k * SEG:(k + 1) * SEG] = gd[k, 0:1, :]
    loss_v[...] = gd[0, 1:2, 0:1]
    stores = [
        pltpu.make_async_copy(src, dst, in_sem.at[i])
        for i, (src, dst) in enumerate(((qg_v, qg_ref), (gg_v, gg_ref), (loss_v, loss_ref)))
    ]
    for store in stores:
        store.start()
    for store in stores:
        store.wait()
    pltpu.make_async_copy(pg_v, pg_ref, in_sem.at[3]).wait()

    for ref, i in (
        (qb.at[:, pl.ds(0, 7 * QB), :], 0), (qb.at[:, pl.ds(0, 8 * QB), :], 1), (far_ref, 2),
        (yr, 4), (dpr, 5), (zs.at[pl.ds(0, 7)], 6),
    ):
        remote(ref, ref, one_s.at[i], one_r.at[i], pp).wait_send()
    for ref, i, n in (
        (stats, 3, 15), (gar, 7, PLANE - 1), (gc, 9, 15), (gd, 10, PLANE - 1)
    ):
        several(ref, i, n).wait_send()


def hand_over(qg_in, pg_in, gg_in, qg_ref, pg_ref, gg_ref, qg_v, pg_v, gg_v, in_sem, out_sem):
    parts = [(qg_in, qg_v, qg_ref), (gg_in, gg_v, gg_ref)]
    for i in range(4):
        at = pl.ds(i * PB // 4, PB // 4)
        parts.append(tuple(ref.at[at, :] for ref in (pg_in, pg_v, pg_ref)))
    loads = [pltpu.make_async_copy(a, b, in_sem.at[i]) for i, (a, b, _) in enumerate(parts)]
    stores = [pltpu.make_async_copy(b, c, out_sem.at[i]) for i, (_, b, c) in enumerate(parts)]
    for load in loads:
        load.start()
    for load, store in zip(loads, stores):
        load.wait()
        store.start()
    for store in stores:
        store.wait()


def on_device(query_hidden, passage_hidden, gain, hard_ids, positive_ids):
    del hard_ids
    hbm = pl.BlockSpec(memory_space=pltpu.HBM)
    any_space = pl.BlockSpec(memory_space=pl.ANY)
    dma = pltpu.SemaphoreType.DMA
    shapes = (
        jax.ShapeDtypeStruct((QB, D), BF16),
        jax.ShapeDtypeStruct((PB, D), BF16),
        jax.ShapeDtypeStruct((1, D), F32),
    )
    query_grad, passage_grad, gain_grad, loss = pl.pallas_call(
        kernel,
        out_shape=(*shapes, jax.ShapeDtypeStruct((1, 1), F32)),
        in_specs=[hbm] * 4,
        out_specs=(any_space,) * 4,
        scratch_shapes=[
            pltpu.VMEM((QB, D), BF16),
            pltpu.VMEM((PB, D), BF16),
            pltpu.VMEM((PB, D), BF16),
            pltpu.VMEM((1, D), F32),
            pltpu.VMEM((1, QB), jnp.int32),
            pltpu.VMEM((NF, NQ, FC), BF16),
            pltpu.VMEM((NF, NP, FC), BF16),
            pltpu.VMEM((NP, NQ), F32),
            pltpu.VMEM((NP, NQ), BF16),
            pltpu.VMEM((NF, NQ, FC), BF16),
            pltpu.VMEM((RING, NF, QB, FC), BF16),
            pltpu.VMEM((RING, NF, QB, FC), BF16),
            pltpu.VMEM((RING, NF, QB, FC), BF16),
            pltpu.VMEM((PB, D), F32),
            pltpu.VMEM((PB, D), BF16),
            pltpu.VMEM((PB, D), BF16),
            pltpu.VMEM((QB, D), F32),
            pltpu.VMEM((2, PB, 1), F32),
            pltpu.VMEM((CLASS, 2, NQ), F32),
            pltpu.VMEM((PLANE, 2, SEG), F32),
            pltpu.VMEM((PLANE, 2, SEG), F32),
            pltpu.VMEM((16, 2, SEG), F32),
            pltpu.VMEM((PLANE, 2, SEG), F32),
            pltpu.VMEM((NQ, NP), BF16),
            pltpu.VMEM((NQ, 1), F32),
            pltpu.VMEM((QB, D), BF16),
            pltpu.VMEM((PB, D), BF16),
            pltpu.VMEM((1, D), F32),
            pltpu.VMEM((1, 1), F32),
            dma((4,)),
            dma((RING, NF)),
            dma((RING, NF)),
            dma((PB // QB,)),
            dma((PB // QB,)),
            dma((NF,)),
            dma((12,)),
            dma((12,)),
        ],
        compiler_params=pltpu.CompilerParams(
            collective_id=0, has_side_effects=True, vmem_limit_bytes=60 * 1024 * 1024
        ),
        cost_estimate=pl.CostEstimate(flops=1_610_612_736, bytes_accessed=2_400_000, transcendentals=200_000),
    )(query_hidden, passage_hidden, gain.reshape(1, D), positive_ids.reshape(1, QB))
    query_grad, passage_grad, gain_grad = pl.pallas_call(
        hand_over,
        out_shape=shapes,
        in_specs=[any_space] * 3,
        out_specs=(any_space,) * 3,
        scratch_shapes=[
            pltpu.VMEM((QB, D), BF16), pltpu.VMEM((PB, D), BF16), pltpu.VMEM((1, D), F32), dma((6,)), dma((6,))
        ],
        compiler_params=pltpu.CompilerParams(vmem_limit_bytes=60 * 1024 * 1024),
    )(query_grad, passage_grad, gain_grad)
    return query_grad, passage_grad, gain_grad.reshape(D), loss.reshape(())


def solution(mesh):
    placed = (
        P(("dx", "dy"), None),
        P(("dx", "dy"), None),
        P(),
        P(("dx", "dy"), None),
        P(("dx", "dy")),
    )
    return jax.shard_map(
        on_device,
        mesh=mesh,
        in_specs=placed,
        out_specs=(P(("dx", "dy"), None), P(("dx", "dy"), None), P(), P()),
        check_vma=False,
    )
```
